512 devices in a mesh: seq: 64 (over x, z), tp: 8 (over y, core).
Axes of the slice: x: 4, y: 4, z: 16, core: 2. Of those that a mesh axis runs over, the one named last changes fastest.
Arguments:
- queries: bfloat16 [8192, 4096], P('seq', 'tp'), may hold values from -128 to 128
- rotated_keys: bfloat16 [8192, 1024], P('seq', 'tp'), may hold values from -4.5 to 4.5
- values: bfloat16 [8192, 1024], P('seq', 'tp'), may hold values from -64 to 64
- decay_rates: float32 [64], P('tp'), may hold values from 2e-06 to 0.016
- decay_codes: int32 [8192, 64], P('seq', 'tp'), may hold values from 1 to 8192
- gate_input: bfloat16 [8192, 4096], P('seq', 'tp'), may hold values from -64 to 64
- norm_gain: float32 [4096], P('tp'), may hold values from 0.1 to 1.9
- bc_weight: bfloat16 [4096, 256], P('tp'), may hold values from -0.09375 to 0.09375
Outputs:
- first_pass: float32 [8192, 4096], P('seq', 'tp')
- second_pass: float32 [8192, 4096], P('seq', 'tp')
The draws below stay inside these ranges and needn't reach their ends.
All inputs are finite; a program needn't handle non-finite values.
Results may differ from the reference program's by a relative error of at most 0.017.
Values may be sent and summed in bfloat16 or wider, within the bound.
A program may use at most 64 MiB of HBM per device.

```python
import math
import jax
import jax.numpy as jnp
from jax import lax

QUERY_HEADS = 32
KEY_VALUE_HEADS = 8
HEAD_SIZE = 128
SH = 64
SP = 64
NS = 128
WINDOW_LENGTH = 2048
STRETCH = 128
TOKENS_PER_SHARD = 128
SERIES_POSITIONS = 8192
WIDTH = 4096


def draw_decay_codes(key, part):
    tier_seed_handle, initial_seed_handle, spike_seed_handle = jax.random.split(jax.random.fold_in(key, 11), 3)
    block_total = SERIES_POSITIONS // TOKENS_PER_SHARD
    levels = jax.random.randint(tier_seed_handle, (block_total, 1, 1), 1, 5)
    raw_codes = jax.random.randint(initial_seed_handle, (block_total, TOKENS_PER_SHARD, SH), 0, 840)
    initial_integers = (raw_codes % (2 * levels) + 1).reshape(SERIES_POSITIONS, SH)
    spike_line_collection = jax.random.permutation(spike_seed_handle, SERIES_POSITIONS)[:3]
    spike_hits = jnp.zeros((SERIES_POSITIONS,), jnp.int32).at[spike_line_collection].set(1)
    return jnp.where(spike_hits[:, None] > 0, SERIES_POSITIONS, initial_integers).astype(jnp.int32)


def draw_decay_rates(key, part):
    slow_key, middle_key, fast_key, pick_key = jax.random.split(jax.random.fold_in(key, 23), 4)
    slow_rates = jax.random.uniform(slow_key, (SH,), jnp.float32, 0.3, 0.6) / (2.0 * SERIES_POSITIONS)
    middle_rates = jnp.exp(jax.random.uniform(middle_key, (SH,), jnp.float32, math.log(0.2), math.log(1.0))) / TOKENS_PER_SHARD
    middle_rates = jnp.minimum(middle_rates, 0.016)
    fast_rates = jnp.exp(jax.random.uniform(fast_key, (SH,), jnp.float32, math.log(0.008), math.log(0.016)))
    fast_share = 0.25
    middle_share = 0.25
    picker = jax.random.uniform(pick_key, (SH,), jnp.float32)
    chosen = jnp.where(picker < fast_share + middle_share, middle_rates, slow_rates)
    return jnp.where(picker < fast_share, fast_rates, chosen)


def shared_keys(key):
    initial_seed_handle = jax.random.fold_in(jax.random.fold_in(key, 41), 0)
    key_lookup_table = jnp.clip(jax.random.normal(initial_seed_handle, (SERIES_POSITIONS, KEY_VALUE_HEADS * HEAD_SIZE), jnp.float32), -4.5, 4.5)
    return key_lookup_table


def draw_rotated_keys(key, part):
    key_lookup_table = shared_keys(key)
    return key_lookup_table.astype(jnp.bfloat16)


def draw_queries(key, part):
    query_table = jnp.clip(jax.random.normal(jax.random.fold_in(key, 43), (SERIES_POSITIONS, QUERY_HEADS * HEAD_SIZE), jnp.float32), -4.5, 4.5)
    return jnp.clip(query_table, -128.0, 128.0).astype(jnp.bfloat16)


def noise_scaled(key, width_total, group_width):
    noise_key, column_key, row_key = jax.random.split(key, 3)
    noise_table = jnp.clip(jax.random.normal(noise_key, (SERIES_POSITIONS, width_total), jnp.float32), -4.5, 4.5)
    column_scale = jnp.exp(jax.random.uniform(column_key, (width_total,), jnp.float32, 0.0, math.log(2.0)))
    row_scale = jnp.exp(jax.random.uniform(row_key, (SERIES_POSITIONS, 1), jnp.float32, 0.0, math.log(2.0)))
    position = (jnp.arange(width_total) // group_width).astype(jnp.float32) / max(width_total // group_width - 1, 1)
    rising = 3.0 ** position
    return jnp.clip(noise_table * column_scale * row_scale * rising, -64.0, 64.0)


def draw_values(key, part):
    return noise_scaled(jax.random.fold_in(key, 53), KEY_VALUE_HEADS * HEAD_SIZE, HEAD_SIZE).astype(jnp.bfloat16)


def draw_gate_input(key, part):
    return noise_scaled(jax.random.fold_in(key, 59), WIDTH, SP).astype(jnp.bfloat16)


def steps_of(key, dims, cuts, low, high):
    def one(dim, blocks):
        heights = jax.random.uniform(jax.random.fold_in(jax.random.fold_in(key, 6), dim), (blocks,), jnp.float32, low / len(cuts), high / len(cuts))
        return jnp.repeat(jnp.exp(heights), dims[dim] // blocks).reshape((-1,) + (1,) * (len(dims) - dim - 1))

    gain = one(*cuts[0])
    for cut in cuts[1:]:
        gain = gain * one(*cut)
    return gain


def noise(stream_key, dims, deviation, limit, cuts=(), kind=jnp.bfloat16):
    level = steps_of(stream_key, dims, cuts, -0.22, 0.18) if cuts else 1.0
    drawn = jax.random.normal(stream_key, dims, jnp.float32) * deviation * level
    return jnp.minimum(jnp.maximum(drawn, -limit), limit).astype(kind)


def setup_inputs(seed: int = 0) -> dict:
    key_of = jax.random.split(jax.random.key(seed), 9)
    queries = draw_queries(jax.random.fold_in(key_of[8], 71), 0)
    rotated_keys = draw_rotated_keys(jax.random.fold_in(key_of[8], 71), 0)
    values = draw_values(jax.random.fold_in(key_of[8], 71), 0)
    decay_rates = draw_decay_rates(jax.random.fold_in(key_of[8], 71), 0)
    decay_codes = draw_decay_codes(jax.random.fold_in(key_of[8], 71), 0)
    gate_input = draw_gate_input(jax.random.fold_in(key_of[8], 71), 0)
    norm_gain = jnp.clip(1.0 + 0.18 * jax.random.normal(key_of[6], (WIDTH,), jnp.float32), 0.1, 1.9)
    bc_weight = noise(key_of[7], (WIDTH, 2 * NS), WIDTH ** -0.5, 0.09375, ((0, 8),))
    return {"queries": queries, "rotated_keys": rotated_keys, "values": values, "decay_rates": decay_rates, "decay_codes": decay_codes, "gate_input": gate_input, "norm_gain": norm_gain, "bc_weight": bc_weight}


EPSILON = 1e-05

def attention(queries, rotated_keys, values):
    group_length = QUERY_HEADS // KEY_VALUE_HEADS
    score_scale = 1.0 / math.sqrt(HEAD_SIZE)
    padding_width = jnp.zeros((WINDOW_LENGTH, KEY_VALUE_HEADS * HEAD_SIZE), rotated_keys.dtype)
    extended_keys = jnp.concatenate([padding_width, rotated_keys], 0)
    extended_values = jnp.concatenate([padding_width, values], 0)
    offsets = jnp.arange(TOKENS_PER_SHARD, dtype=jnp.int32)
    key_offsets = jnp.arange(WINDOW_LENGTH + TOKENS_PER_SHARD, dtype=jnp.int32)

    def one_block(block_no):
        leading_row = (block_no * TOKENS_PER_SHARD).astype(jnp.int32)
        query_row_block = lax.dynamic_slice_in_dim(queries, leading_row, TOKENS_PER_SHARD, 0).reshape(TOKENS_PER_SHARD, KEY_VALUE_HEADS, group_length, HEAD_SIZE)
        key_row_block = lax.dynamic_slice_in_dim(extended_keys, leading_row, WINDOW_LENGTH + TOKENS_PER_SHARD, 0).reshape(WINDOW_LENGTH + TOKENS_PER_SHARD, KEY_VALUE_HEADS, HEAD_SIZE)
        value_row_block = lax.dynamic_slice_in_dim(extended_values, leading_row, WINDOW_LENGTH + TOKENS_PER_SHARD, 0).reshape(WINDOW_LENGTH + TOKENS_PER_SHARD, KEY_VALUE_HEADS, HEAD_SIZE)
        scores = jnp.einsum('tkgd,skd->kgts', query_row_block.astype(jnp.float32), key_row_block.astype(jnp.float32), precision=lax.Precision.HIGHEST) * score_scale
        query_pos = leading_row + offsets
        key_pos = leading_row - WINDOW_LENGTH + key_offsets
        allowed = (key_pos[None, :] <= query_pos[:, None]) & (key_pos[None, :] > query_pos[:, None] - WINDOW_LENGTH) & (key_pos[None, :] >= 0)
        scores = jnp.where(allowed[None, None], scores, -jnp.inf)
        row_max = lax.optimization_barrier(jnp.max(scores, axis=3, keepdims=True))
        exponent = jnp.exp(scores - row_max)
        probs = (exponent / lax.optimization_barrier(jnp.sum(exponent, axis=3, keepdims=True))).astype(jnp.bfloat16)
        mixed_rows = jnp.einsum('kgts,skd->tkgd', probs.astype(jnp.float32), value_row_block.astype(jnp.float32), precision=lax.Precision.HIGHEST)
        return mixed_rows.astype(jnp.bfloat16).reshape(TOKENS_PER_SHARD, QUERY_HEADS * HEAD_SIZE)
    blocks_out = lax.map(one_block, jnp.arange(SERIES_POSITIONS // TOKENS_PER_SHARD, dtype=jnp.int32))
    return blocks_out.reshape(SERIES_POSITIONS, QUERY_HEADS * HEAD_SIZE)

def core(inputs, decay_rates, decay_codes, gate_input, norm_gain, bc_weight):
    as_float = inputs.astype(jnp.float32)
    spread = jnp.sqrt(lax.optimization_barrier(jnp.mean(as_float * as_float, axis=1, keepdims=True)) + EPSILON)
    normed = (as_float / spread).astype(jnp.bfloat16)
    projected = (jnp.dot(inputs, bc_weight, preferred_element_type=jnp.float32) / spread).astype(jnp.bfloat16)
    stretch_count = SERIES_POSITIONS // STRETCH
    x_stretches = normed.reshape(stretch_count, STRETCH, SH, SP)
    b_stretches = projected[:, :NS].reshape(stretch_count, STRETCH, NS)
    c_stretches = projected[:, NS:].reshape(stretch_count, STRETCH, NS)
    code_stretches = decay_codes.reshape(stretch_count, STRETCH, SH)
    lower_mask = (jnp.arange(STRETCH)[:, None] >= jnp.arange(STRETCH)[None, :])[:, :, None]

    def advance(state, pieces):
        x_block, b_block, c_block, code_block = pieces
        ell = -decay_rates[None, :] * jnp.cumsum(code_block, axis=0, dtype=jnp.int32).astype(jnp.float32)
        gram_matrix = jnp.dot(c_block, b_block.T, preferred_element_type=jnp.float32)
        decay_gaps = jnp.where(lower_mask, ell[:, None, :] - ell[None, :, :], 0.0)
        mixing = jnp.where(lower_mask, gram_matrix[:, :, None] * jnp.exp(decay_gaps), 0.0).astype(jnp.bfloat16)
        y_local = jnp.einsum('tsh,shp->thp', mixing.astype(jnp.float32), x_block.astype(jnp.float32), precision=lax.Precision.HIGHEST)
        tail_decay = jnp.exp(ell[-1][None, :] - ell)
        b_weighted = (b_block.astype(jnp.float32)[:, None, :] * tail_decay[:, :, None]).astype(jnp.bfloat16)
        contrib = jnp.einsum('shn,shp->hnp', b_weighted.astype(jnp.float32), x_block.astype(jnp.float32), precision=lax.Precision.HIGHEST)
        c_weighted = c_block.astype(jnp.float32)[:, None, :] * jnp.exp(ell)[:, :, None]
        y_carried = jnp.einsum('thn,hnp->thp', c_weighted, state, precision=lax.Precision.HIGHEST)
        new_state = jnp.exp(ell[-1])[:, None, None] * state + contrib
        return (new_state, y_local + y_carried)
    start_state = jnp.zeros((SH, NS, SP), jnp.float32)
    final_state, y_blocks = lax.scan(advance, start_state, (x_stretches, b_stretches, c_stretches, code_stretches))
    y_all = y_blocks.reshape(SERIES_POSITIONS, SH * SP)
    gated_out = y_all * jax.nn.silu(gate_input.astype(jnp.float32))
    out_scale = jnp.sqrt(lax.optimization_barrier(jnp.mean(gated_out * gated_out, axis=1, keepdims=True)) + EPSILON)
    return gated_out / out_scale * norm_gain

def reference(queries, rotated_keys, values, decay_rates, decay_codes, gate_input, norm_gain, bc_weight):
    attended = attention(queries, rotated_keys, values)
    first_pass = core(attended, decay_rates, decay_codes, gate_input, norm_gain, bc_weight)
    pass_input = first_pass.astype(jnp.bfloat16)
    second_pass = core(pass_input, decay_rates, decay_codes, gate_input, norm_gain, bc_weight)
    return (first_pass, second_pass)
```

```python
import functools
import math

import jax
import jax.numpy as jnp
from jax import lax
from jax.experimental import pallas as pl
from jax.experimental.pallas import tpu as pltpu
from jax.sharding import PartitionSpec as P

HEADS = 4
HS = 128
NH = 8
PAIRS = NH // 2
ROWS = 128
REACH = 16
NZ = 16
NX = 4
NT = 8
CHANNELS = 4096
COLS = 512
EPS = 1e-5
SLICE = 32
BF = jnp.bfloat16
F32 = jnp.float32
MESH = pl.DeviceIdType.MESH
NEG = -1e30
FIRST = (3, 13, 1, 15, 16)
RELAY = {3: (6, 4, 2), 13: (10, 14, 12), 6: (8, 7, 5), 10: (9, 11)}
NEAR = (1, 2, 3, 13, 15)


def dot(a, b, ca=1, cb=0):
    return lax.dot_general(a, b, (((ca,), (cb,)), ((), ())), preferred_element_type=F32)


def split(a):
    hi = a.astype(BF).astype(F32)
    return hi, a - hi


def rows4(a):
    return jnp.concatenate([a] * 4, 0)


def pack4(a, b, lane):
    ah, al = split(a)
    bh, bl = split(b)
    return jnp.where(lane < 64, jnp.where(lane < 32, ah, al), jnp.where(lane < 96, bh, bl))


def unpack4(v):
    return v[:, 0:1] + v[:, 32:33], v[:, 64:65] + v[:, 96:97]


def kernel(
    q_hbm, k_hbm, v_hbm, rates, codes_hbm, gate_hbm, gain_hbm, w_hbm,
    out1, out2,
    q_s, k_s, v_s, codes_s, gate_s, gain_s, w_s,
    sc_s, m_s, l_s, decay_s, tail_s, expell_s, silu_s,
    dexp_s, dz_s, dp_s,
    x_s, gated_s, y_s,
    pay_s, rs_s, agsrc_s, ag_s,
    cb_s, e1_s, pre_s, tsrc_s, t_s, e3src_s, st_s,
    gsrc_s, g_s,
    in_sem,
    kv_ss, kv_rs, d_ss, d_rs,
    rs_ss, rs_rs, ag_ss, ag_rs,
    e1_ss, e1_rs, t_ss, t_rs, e3_ss, e3_rs,
    g_ss, g_rs,
):
    s = lax.axis_index("seq")
    t = lax.axis_index("tp")
    x = lax.div(s, NZ)
    z = lax.rem(s, NZ)

    def zpeer(j):
        o = lax.rem(z + j, NZ)
        return o, (x * NZ + o, t)

    def xpeer(j):
        o = lax.rem(x + j, NX)
        return o, (o * NZ + z, t)

    def tpeer(j):
        o = lax.rem(t + j, NT)
        return o, (s, o)

    def remote(src, dst, ss, rs, dev):
        return pltpu.make_async_remote_copy(
            src_ref=src, dst_ref=dst, send_sem=ss, recv_sem=rs, device_id=dev, device_id_type=MESH
        )

    def each(n, body):
        def step(j, c):
            body(j)
            return c

        lax.fori_loop(1, n, step, 0)

    loads = [
        pltpu.make_async_copy(src, dst, in_sem.at[i])
        for i, (src, dst) in enumerate(
            (
                (codes_hbm, codes_s),
                (q_hbm, q_s),
                (k_hbm, k_s.at[0]),
                (v_hbm, v_s.at[0]),
                (gate_hbm, gate_s),
                (gain_hbm, gain_s.at[0]),
                (w_hbm, w_s),
            )
        )
    ]
    for c in loads:
        c.start()

    barrier = pltpu.get_barrier_semaphore()

    def greet(dev):
        pl.semaphore_signal(barrier, inc=1, device_id=dev, device_id_type=MESH)

    def block_device(k):
        return (lax.rem(s + (k + NX * NZ), NX * NZ), t)

    for k in NEAR:
        greet(block_device(k))
        greet(block_device(-k))
    each(NX, lambda j: greet(xpeer(j)[1]))
    each(NZ, lambda j: greet(zpeer(j)[1]))
    each(NT, lambda j: greet(tpeer(j)[1]))

    row = lax.broadcasted_iota(jnp.int32, (ROWS, ROWS), 0)
    col = lax.broadcasted_iota(jnp.int32, (ROWS, ROWS), 1)
    lane1 = lax.broadcasted_iota(jnp.int32, (1, 128), 1)
    lower = row >= col
    upper = jnp.where(row <= col, 1.0, 0.0).astype(BF)
    loads[0].wait()
    codes = codes_s[...]
    code_hi = lax.shift_right_logical(codes, 7).astype(F32).astype(BF)
    code_lo = (codes & 127).astype(F32).astype(BF)
    cum_rows = dot(code_hi, upper) * 128.0 + dot(code_lo, upper)
    cum = jnp.transpose(jnp.concatenate([cum_rows, jnp.zeros((128 - NH, ROWS), F32)], 0))
    for hp in range(PAIRS):
        tails, ells, ends = [], [], []
        for h in (2 * hp, 2 * hp + 1):
            rate = -rates[h]
            ell = cum[:, h : h + 1] * rate
            ell_row = cum_rows[h : h + 1, :] * rate
            end = ell[ROWS - 1 :, :]
            gap = jnp.where(lower, ell - ell_row, 0.0)
            decay_s[h] = jnp.where(lower, jnp.exp(gap), 0.0)
            tails.append(jnp.exp(end - ell))
            ells.append(jnp.exp(ell))
            ends.append(jnp.exp(end))
        cs = slice(hp * 128, hp * 128 + 128)
        tail_s[:, cs] = jnp.where(col < 64, tails[0], tails[1])
        expell_s[:, cs] = jnp.where(col < 64, ells[0], ells[1])
        dexp_s[hp] = jnp.broadcast_to(jnp.where(lane1 < 64, ends[0], ends[1]), (8, 128))

    loads[1].wait()
    loads[2].wait()
    loads[3].wait()
    scale = math.log2(math.e) / math.sqrt(HS)
    diff = col - row
    own_k = k_s[0]
    for h in range(HEADS):
        qh = q_s[:, h * HS : (h + 1) * HS]
        sc = jnp.where(lower, dot(qh, own_k, 1, 1), NEG)
        m = jnp.max(sc, axis=1, keepdims=True)
        m_s[h] = jnp.broadcast_to(m, (ROWS, HS))
        l_s[h] = jnp.exp2((sc - m) * scale)
        sc_s[0, h] = sc

    loads[4].wait()
    g = gate_s[...].astype(F32)
    silu_s[...] = g / (1.0 + jnp.exp(-g))

    pl.semaphore_wait(barrier, 2 * len(NEAR) + (NX - 1) + (NZ - 1) + (NT - 1))

    def hop(i, a, b):
        buf = (k_s, v_s)[i]
        return remote(buf.at[a], buf.at[b], kv_ss.at[i, b], kv_rs.at[i, b], block_device(b - a))

    def arrived(i, b):
        hop(i, b - 1, b).wait_recv()

    for i in range(2):
        for b in FIRST:
            hop(i, 0, b).start()

    def d_send(j):
        o, dev = zpeer(j)
        remote(dexp_s.at[lax.div(o, 4)], dz_s.at[z], d_ss.at[o], d_rs.at[z], dev).start()

    each(NZ, d_send)
    dz_s[z] = dexp_s[lax.div(z, 4)]

    def d_wait(j):
        o, dev = zpeer(j)
        remote(dexp_s.at[0], dz_s.at[o], d_ss.at[o], d_rs.at[o], dev).wait_recv()

    def decay_products():
        each(NZ, d_wait)
        running = jnp.ones((8, 128), F32)
        for zz in range(NZ):
            dp_s[zz] = running
            running = running * dz_s[zz]
        for p in range(2):
            tsrc_s[p, SLICE:] = running

    def relay(a):
        for i in range(2):
            arrived(i, a)
            for b in RELAY[a]:
                hop(i, a, b).start()

    def come(*slots):
        for b in slots:
            arrived(0, b)
            arrived(1, b)

    def attend(a, b):
        big = jnp.int32(1 << 20)

        def limit(k):
            return jnp.where(s >= k, jnp.int32((k - REACH) * ROWS), big)

        keys = jnp.concatenate([k_s[a], k_s[b]], 0)
        ok = jnp.concatenate([diff > limit(a), diff > limit(b)], 1)
        for h in range(HEADS):
            qh = q_s[:, h * HS : (h + 1) * HS]
            sc = jnp.where(ok, dot(qh, keys, 1, 1), NEG)
            old = m_s[h]
            m = jnp.maximum(old, jnp.max(sc, axis=1, keepdims=True))
            alpha = jnp.exp2((old - m) * scale)
            mm = jnp.concatenate([m, m], 1)
            p = jnp.exp2((sc - mm) * scale)
            m_s[h] = m
            l_s[h] = l_s[h] * alpha + (p[:, :HS] + p[:, HS:])
            sc_s[a, h] = sc[:, :HS]
            sc_s[b, h] = sc[:, HS:]

    relay(3)
    relay(13)
    decay_products()
    come(1, 15)
    attend(1, 15)
    attend(3, 13)
    relay(6)
    relay(10)
    come(16, 2, 4, 14, 12)
    attend(2, 16)
    attend(4, 14)
    attend(6, 12)
    come(5)
    attend(5, 10)
    come(7, 11)
    attend(7, 11)
    come(8, 9)
    attend(8, 9)
    for h in range(HEADS):
        m = m_s[h]
        inv = 1.0 / jnp.sum(l_s[h], axis=1, keepdims=True)
        mixed = jnp.zeros((ROWS, HS), F32)
        for a in range(0, REACH, 2):
            parts = [(jnp.exp2((sc_s[k, h] - m) * scale) * inv).astype(BF) for k in (a, a + 1)]
            mixed = mixed + dot(jnp.concatenate(parts, 1), v_s[a : a + 2].reshape(2 * ROWS, HS))
        last = (jnp.exp2((sc_s[REACH, h] - m) * scale) * inv).astype(BF)
        mixed = mixed + dot(last, v_s[REACH])
        x_s[:, h * HS : (h + 1) * HS] = mixed.astype(BF)

    loads[5].wait()
    loads[6].wait()

    def kv_done():
        for i in range(2):
            for b in FIRST:
                hop(i, 0, b).wait_send()
            for a, bs in RELAY.items():
                for b in bs:
                    hop(i, a, b).wait_send()

    def d_done(j):
        o, dev = zpeer(j)
        remote(dexp_s.at[0], dz_s.at[z], d_ss.at[o], d_rs.at[z], dev).wait_send()

    def z_done(p):
        def body(j):
            o, dev = zpeer(j)
            remote(cb_s.at[p, o], e1_s.at[p, z], e1_ss.at[p, o], e1_rs.at[p, z], dev).wait_send()
            remote(e3src_s.at[p, o], st_s.at[p, z], e3_ss.at[p, o], e3_rs.at[p, z], dev).wait_send()

        return body

    def x_done(p):
        def body(j):
            o, dev = xpeer(j)
            remote(tsrc_s.at[p], t_s.at[p, x], t_ss.at[p, o], t_rs.at[p, x], dev).wait_send()

        return body

    def t_done(p):
        def body(j):
            o, dev = tpeer(j)
            remote(pay_s.at[p, o], rs_s.at[p, t], rs_ss.at[p, o], rs_rs.at[p, t], dev).wait_send()
            remote(agsrc_s.at[p], ag_s.at[p, t], ag_ss.at[p, o], ag_rs.at[p, t], dev).wait_send()

        return body

    def g_done(j):
        o, dev = tpeer(j)
        remote(gsrc_s, g_s.at[t], g_ss.at[o], g_rs.at[t], dev).wait_send()

    lane16 = lax.broadcasted_iota(jnp.int32, (16, 128), 1)

    for p in range(2):
        if p == 0:
            xb = x_s[...]
            xf = xb.astype(F32)
            s1 = s2 = jnp.sum(xf * xf, axis=1, keepdims=True)
        else:
            gv = gated_s[...]
            s1 = jnp.sum(gv * gv, axis=1, keepdims=True)
            gg = gv * gain_s[...]
            s2 = jnp.sum(gg * gg, axis=1, keepdims=True)
            xb = gg.astype(BF)
        partial = jnp.concatenate([dot(xb, w_s[...]), pack4(s1, s2, col)], 1)
        pay_s[p] = partial.reshape(NT, 16, 384)

        def rs_send(j, p=p):
            o, dev = tpeer(j)
            remote(pay_s.at[p, o], rs_s.at[p, t], rs_ss.at[p, o], rs_rs.at[p, t], dev).start()

        def rs_wait(j, p=p):
            o, dev = tpeer(j)
            remote(pay_s.at[p, o], rs_s.at[p, o], rs_ss.at[p, o], rs_rs.at[p, o], dev).wait_recv()

        each(NT, rs_send)
        rs_s[p, t] = pay_s[p, t]
        each(NT, rs_wait)
        tot = jnp.sum(rs_s[p], axis=0)
        q1, q2 = unpack4(tot[:, 256:])
        if p == 0:
            scale1 = jnp.ones_like(q1)
        else:
            scale1 = jnp.sqrt(q1 * (1.0 / CHANNELS) + EPS)
        spread = jnp.sqrt(q2 / (scale1 * scale1) * (1.0 / CHANNELS) + EPS)
        proj = tot[:, :256] / (scale1 * spread)
        own = jnp.concatenate([proj, pack4(scale1, spread, lane16)], 1).astype(BF)
        agsrc_s[p] = own
        ag_s[p, t] = own

        def ag_send(j, p=p):
            o, dev = tpeer(j)
            remote(agsrc_s.at[p], ag_s.at[p, t], ag_ss.at[p, o], ag_rs.at[p, t], dev).start()

        def ag_wait(j, p=p):
            o, dev = tpeer(j)
            remote(agsrc_s.at[p], ag_s.at[p, o], ag_ss.at[p, o], ag_rs.at[p, o], dev).wait_recv()

        each(NT, ag_send)
        each(NT, ag_wait)
        agv = ag_s[p].reshape(ROWS, 384)
        b_in = agv[:, :128]
        c_out = agv[:, 128:256]
        scale1, spread = unpack4(agv[:, 256:].astype(F32))
        if p == 1:
            f1 = gated_s[...] * (1.0 / scale1) * gain_s[...]
            out1[...] = f1
            xf = f1.astype(BF).astype(F32)
        xn = (xf * (1.0 / spread)).astype(BF)

        b_rows = jnp.transpose(b_in.astype(F32)).astype(BF)
        contrib = dot(b_rows, (xn.astype(F32) * tail_s[...]).astype(BF)).astype(BF)
        for o in range(NZ):
            hp, nq = o // 4, o % 4
            cb_s[p, o] = contrib[nq * SLICE : (nq + 1) * SLICE, hp * 128 : (hp + 1) * 128]

        def e1_send(j, p=p):
            o, dev = zpeer(j)
            remote(cb_s.at[p, o], e1_s.at[p, z], e1_ss.at[p, o], e1_rs.at[p, z], dev).start()

        def e1_wait(j, p=p):
            o, dev = zpeer(j)
            remote(cb_s.at[p, o], e1_s.at[p, o], e1_ss.at[p, o], e1_rs.at[p, o], dev).wait_recv()

        each(NZ, e1_send)
        e1_s[p, z] = cb_s[p, z]

        gram = dot(c_out, b_rows)
        for hp in range(PAIRS):
            cs = slice(hp * 128, hp * 128 + 128)
            mix = jnp.concatenate([gram * decay_s[2 * hp], gram * decay_s[2 * hp + 1]], 1).astype(BF)
            xp = xn[:, cs]
            zero = jnp.zeros_like(xp)
            both = jnp.concatenate([jnp.where(col < 64, xp, zero), jnp.where(col < 64, zero, xp)], 0)
            y_s[:, cs] = dot(mix, both)

        if p == 0:
            kv_done()
            each(NZ, d_done)
        else:
            each(NZ, z_done(0))
            each(NX, x_done(0))
            each(NT, t_done(0))
        each(NZ, e1_wait)
        state = jnp.zeros((SLICE, 128), F32)
        for zz in range(NZ):
            pre_s[zz] = state
            state = rows4(dz_s[zz]) * state + e1_s[p, zz].astype(F32)
        tsrc_s[p, :SLICE] = state
        t_s[p, x] = tsrc_s[p]

        def t_send(j, p=p):
            o, dev = xpeer(j)
            remote(tsrc_s.at[p], t_s.at[p, x], t_ss.at[p, o], t_rs.at[p, x], dev).start()

        def t_wait(j, p=p):
            o, dev = xpeer(j)
            remote(tsrc_s.at[p], t_s.at[p, o], t_ss.at[p, o], t_rs.at[p, o], dev).wait_recv()

        each(NX, t_send)
        each(NX, t_wait)
        before = jnp.zeros((SLICE, 128), F32)
        for xx in range(NX - 1):
            before = jnp.where(xx < x, rows4(t_s[p, xx, SLICE:]) * before + t_s[p, xx, :SLICE], before)
        for zz in range(NZ):
            e3src_s[p, zz] = (pre_s[zz] + rows4(dp_s[zz]) * before).astype(BF)

        def e3_send(j, p=p):
            o, dev = zpeer(j)
            remote(e3src_s.at[p, o], st_s.at[p, z], e3_ss.at[p, o], e3_rs.at[p, z], dev).start()

        def e3_wait(j, p=p):
            o, dev = zpeer(j)
            remote(e3src_s.at[p, o], st_s.at[p, o], e3_ss.at[p, o], e3_rs.at[p, o], dev).wait_recv()

        each(NZ, e3_send)
        st_s[p, z] = e3src_s[p, z]
        each(NZ, e3_wait)
        for hp in range(PAIRS):
            cs = slice(hp * 128, hp * 128 + 128)
            st = st_s[p, 4 * hp : 4 * hp + 4].reshape(128, 128)
            y = y_s[:, cs] + dot(c_out, st) * expell_s[:, cs]
            gated_s[:, cs] = y * silu_s[:, cs]

    gv = gated_s[...]
    hi, lo = split(gv * gv)
    ones8 = jnp.ones((8, COLS), BF)
    mine = dot(ones8, hi.astype(BF), 1, 1) + dot(ones8, lo.astype(BF), 1, 1)
    gsrc_s[...] = mine
    g_s[t] = mine

    def g_send(j):
        o, dev = tpeer(j)
        remote(gsrc_s, g_s.at[t], g_ss.at[o], g_rs.at[t], dev).start()

    def g_wait(j):
        o, dev = tpeer(j)
        remote(gsrc_s, g_s.at[o], g_ss.at[o], g_rs.at[o], dev).wait_recv()

    each(NT, g_send)
    each(NZ, z_done(1))
    each(NX, x_done(1))
    each(NT, t_done(1))
    each(NT, g_wait)
    total = jnp.sum(g_s[...], axis=0)[0:1, :]
    inv = lax.rsqrt(total * (1.0 / CHANNELS) + EPS)
    inv = jnp.transpose(jnp.broadcast_to(inv, (128, 128)))
    for hp in range(PAIRS):
        cs = slice(hp * 128, hp * 128 + 128)
        out2[:, cs] = gated_s[:, cs] * inv * gain_s[:, cs]
    each(NT, g_done)


def on_device(
    queries, rotated_keys, values, decay_rates, decay_codes, gate_input, norm_gain, bc_weight
):
    vm = pltpu.VMEM
    dma = pltpu.SemaphoreType.DMA
    anyspace = pl.BlockSpec(memory_space=pl.ANY)
    block = vm((ROWS, COLS), F32)
    scratch = [
        vm((ROWS, COLS), BF),
        vm((REACH + 1, ROWS, HS), BF),
        vm((REACH + 1, ROWS, HS), BF),
        vm((NH, ROWS), jnp.int32),
        vm((ROWS, COLS), BF),
        vm((1, COLS), F32),
        vm((COLS, 256), BF),
        vm((REACH + 1, HEADS, ROWS, HS), F32),
        vm((HEADS, ROWS, HS), F32),
        vm((HEADS, ROWS, HS), F32),
        vm((NH, ROWS, ROWS), F32),
        vm((ROWS, COLS), F32),
        vm((ROWS, COLS), F32),
        vm((ROWS, COLS), F32),
        vm((PAIRS, 8, 128), F32),
        vm((NZ, 8, 128), F32),
        vm((NZ, 8, 128), F32),
        vm((ROWS, COLS), BF),
        vm((ROWS, COLS), F32),
        vm((ROWS, COLS), F32),
        vm((2, NT, 16, 384), F32),
        vm((2, NT, 16, 384), F32),
        vm((2, 16, 384), BF),
        vm((2, NT, 16, 384), BF),
        vm((2, NZ, SLICE, 128), BF),
        vm((2, NZ, SLICE, 128), BF),
        vm((NZ, SLICE, 128), F32),
        vm((2, SLICE + 8, 128), F32),
        vm((2, NX, SLICE + 8, 128), F32),
        vm((2, NZ, SLICE, 128), BF),
        vm((2, NZ, SLICE, 128), BF),
        vm((8, 128), F32),
        vm((NT, 8, 128), F32),
        dma((7,)),
        dma((2, REACH + 1)), dma((2, REACH + 1)),
        dma((NZ,)), dma((NZ,)),
        dma((2, NT)), dma((2, NT)), dma((2, NT)), dma((2, NT)),
        dma((2, NZ)), dma((2, NZ)), dma((2, NX)), dma((2, NX)), dma((2, NZ)), dma((2, NZ)),
        dma((NT,)), dma((NT,)),
    ]
    return pl.pallas_call(
        kernel,
        out_shape=(block, block),
        in_specs=[anyspace] * 3 + [pl.BlockSpec(memory_space=pltpu.SMEM)] + [anyspace] * 4,
        out_specs=(pl.BlockSpec(memory_space=vm),) * 2,
        scratch_shapes=scratch,
        compiler_params=pltpu.CompilerParams(
            collective_id=0, has_side_effects=True, vmem_limit_bytes=60 << 20
        ),
    )(queries, rotated_keys, values, decay_rates, decay_codes.T, gate_input, norm_gain, bc_weight)


def solution(mesh):
    return jax.shard_map(
        on_device,
        mesh=mesh,
        in_specs=(
            P("seq", "tp"),
            P("seq", "tp"),
            P("seq", "tp"),
            P("tp"),
            P("seq", "tp"),
            P("seq", "tp"),
            P("tp"),
            P("tp", None),
        ),
        out_specs=(P("seq", "tp"), P("seq", "tp")),
        check_vma=False,
    )
```

```python
import functools
import math

import jax
import jax.numpy as jnp
from jax import lax
from jax.experimental import pallas as pl
from jax.experimental.pallas import tpu as pltpu
from jax.sharding import PartitionSpec as P

HEADS = 4
HS = 128
NH = 8
PAIRS = NH // 2
ROWS = 128
REACH = 16
NZ = 16
NX = 4
NT = 8
NY = 4
HALF = 64
CHANNELS = 4096
COLS = 512
EPS = 1e-5
SLICE = 16
BF = jnp.bfloat16
F32 = jnp.float32
MESH = pl.DeviceIdType.MESH
NEG = -1e30
FIRST = (3, 13, 1, 15, 16)
RELAY = {3: (6, 4, 2), 13: (10, 14, 12), 6: (8, 7, 5), 10: (9, 11)}
NEAR = (1, 2, 3, 13, 15)


def dot(a, b, ca=1, cb=0):
    return lax.dot_general(a, b, (((ca,), (cb,)), ((), ())), preferred_element_type=F32)


def split(a):
    hi = a.astype(BF).astype(F32)
    return hi, a - hi


def pack4(a, b, lane):
    ah, al = split(a)
    bh, bl = split(b)
    return jnp.where(lane < 64, jnp.where(lane < 32, ah, al), jnp.where(lane < 96, bh, bl))


def unpack4(v):
    return v[:, 0:1] + v[:, 32:33], v[:, 64:65] + v[:, 96:97]


def kernel(
    q_hbm, k_hbm, v_hbm, rates, codes_hbm, gate_hbm, gain_hbm, w_hbm,
    out1, out2,
    q_s, k_s, v_s, codes_s, gate_s, gain_s, w_s,
    sc_s, m_s, l_s, decay_s, tail_s, expell_s, silu_s,
    dexp_s, dz_s, dp_s,
    x_s, gated_s, y_s,
    pay_s, pr_s, ysrc_s, rs_s, ag_s,
    cb_s, e1_s, pre_s, tsrc_s, t_s, e3src_s, st_s,
    gsrc_s, g_s,
    in_sem,
    kv_ss, kv_rs, d_ss, d_rs,
    pair_ss, pair_rs, rs_ss, rs_rs, ag_ss, ag_rs,
    e1_ss, e1_rs, t_ss, t_rs, e3_ss, e3_rs,
    g_ss, g_rs,
):
    s = lax.axis_index("seq")
    t = lax.axis_index("tp")
    x = lax.div(s, NZ)
    z = lax.rem(s, NZ)
    chip = lax.div(t, 2)
    core = lax.rem(t, 2)
    partner = (s, t + 1 - 2 * core)

    def zpeer(j):
        o = lax.rem(z + j, NZ)
        return o, (x * NZ + o, t)

    def xpeer(j):
        o = lax.rem(x + j, NX)
        return o, (o * NZ + z, t)

    def tpeer(j):
        o = lax.rem(t + j, NT)
        return o, (s, o)

    def ypeer(j):
        o = lax.rem(chip + j, NY)
        return o, (s, 2 * o + core)

    def remote(src, dst, ss, rs, dev):
        return pltpu.make_async_remote_copy(
            src_ref=src, dst_ref=dst, send_sem=ss, recv_sem=rs, device_id=dev, device_id_type=MESH
        )

    def all_in(ref, sem):
        remote(ref, ref, sem, sem, partner).wait_recv()

    def all_out(ref, sem):
        remote(ref, ref, sem, sem, partner).wait_send()

    def each(n, body):
        def step(j, c):
            body(j)
            return c

        lax.fori_loop(1, n, step, 0)

    barrier = pltpu.get_barrier_semaphore()

    def greet(dev):
        pl.semaphore_signal(barrier, inc=1, device_id=dev, device_id_type=MESH)

    def block_device(k):
        return (lax.rem(s + (k + NX * NZ), NX * NZ), t)

    for k in NEAR:
        greet(block_device(k))
        greet(block_device(-k))
    each(NX, lambda j: greet(xpeer(j)[1]))
    each(NZ, lambda j: greet(zpeer(j)[1]))
    each(NT, lambda j: greet(tpeer(j)[1]))

    loads = [
        pltpu.make_async_copy(src, dst, in_sem.at[i])
        for i, (src, dst) in enumerate(
            (
                (k_hbm, k_s.at[0]),
                (v_hbm, v_s.at[0]),
                (codes_hbm, codes_s),
                (q_hbm, q_s),
                (gate_hbm, gate_s),
                (gain_hbm, gain_s.at[0]),
                (w_hbm, w_s),
            )
        )
    ]
    for c in loads:
        c.start()

    pl.semaphore_wait(barrier, 2 * len(NEAR) + (NX - 1) + (NZ - 1) + (NT - 1))

    def hop(i, a, b):
        buf = (k_s, v_s)[i]
        return remote(buf.at[a], buf.at[b], kv_ss.at[i, b], kv_rs.at[i, b], block_device(b - a))

    def arrived(i, b):
        hop(i, b - 1, b).wait_recv()

    loads[0].wait()
    loads[1].wait()
    for group in (FIRST[:2], FIRST[2:]):
        for i in range(2):
            for b in group:
                hop(i, 0, b).start()

    row = lax.broadcasted_iota(jnp.int32, (ROWS, ROWS), 0)
    col = lax.broadcasted_iota(jnp.int32, (ROWS, ROWS), 1)
    lane1 = lax.broadcasted_iota(jnp.int32, (1, 128), 1)
    lower = row >= col
    upper = jnp.where(row <= col, 1.0, 0.0).astype(BF)
    loads[2].wait()
    codes = codes_s[...]
    code_hi = lax.shift_right_logical(codes, 7).astype(F32).astype(BF)
    code_lo = (codes & 127).astype(F32).astype(BF)
    cum_rows = dot(code_hi, upper) * 128.0 + dot(code_lo, upper)
    cum = jnp.transpose(jnp.concatenate([cum_rows, jnp.zeros((128 - NH, ROWS), F32)], 0))
    for hp in range(PAIRS):
        ells, ends = [], []
        for h in (2 * hp, 2 * hp + 1):
            rate = -rates[h]
            ell = cum[:, h : h + 1] * rate
            ell_row = cum_rows[h : h + 1, :] * rate
            end = ell[ROWS - 1 :, :]
            gap = jnp.where(lower, ell - ell_row, 0.0)
            decay_s[h] = jnp.where(lower, jnp.exp(gap), 0.0)
            tail_s[h : h + 1, :] = jnp.exp(end - ell_row)
            ells.append(jnp.exp(ell))
            ends.append(jnp.exp(end))
        cs = slice(hp * 128, hp * 128 + 128)
        expell_s[:, cs] = jnp.where(col < 64, ells[0], ells[1])
        dexp_s[hp % 2, hp // 2 : hp // 2 + 1, :] = jnp.where(lane1 < 64, ends[0], ends[1])

    def d_send(j):
        o, dev = zpeer(j)
        remote(dexp_s.at[lax.div(o, 8)], dz_s.at[z], d_ss, d_rs, dev).start()

    each(NZ, d_send)
    dz_s[z] = dexp_s[lax.div(z, 8)]

    loads[3].wait()
    scale = math.log2(math.e) / math.sqrt(HS)
    diff = col - row
    own_k = k_s[0]
    for h in range(HEADS):
        qh = q_s[:, h * HS : (h + 1) * HS]
        sc = jnp.where(lower, dot(qh, own_k, 1, 1), NEG)
        m = jnp.max(sc, axis=1, keepdims=True)
        m_s[h] = jnp.broadcast_to(m, (ROWS, HS))
        l_s[h] = jnp.exp2((sc - m) * scale)
        sc_s[0, h] = sc

    loads[4].wait()
    g = gate_s[...].astype(F32)
    silu_s[...] = g / (1.0 + jnp.exp(-g))

    def decay_products():
        all_in(dz_s.at[pl.ds(0, NZ - 1)], d_rs)
        running = jnp.ones((2, 128), F32)
        for zz in range(NZ):
            dp_s[zz] = running
            running = running * dz_s[zz]
        for p in range(2):
            for half in range(2):
                tsrc_s[2 * p + half, SLICE:] = jnp.broadcast_to(running[half : half + 1], (8, 128))

    def relay(a, b):
        for i in range(2):
            for k in (a, b):
                arrived(i, k)
                hop(i, k, RELAY[k][0]).start()
        for n in (1, 2):
            for k in (a, b):
                for i in range(2):
                    for to in RELAY[k][n : n + 1]:
                        hop(i, k, to).start()

    def come(*slots):
        for b in slots:
            arrived(0, b)
            arrived(1, b)

    def attend(a, b):
        big = jnp.int32(1 << 20)

        def limit(k):
            return jnp.where(s >= k, jnp.int32((k - REACH) * ROWS), big)

        keys = jnp.concatenate([k_s[a], k_s[b]], 0)
        ok = jnp.concatenate([diff > limit(a), diff > limit(b)], 1)
        for h in range(HEADS):
            qh = q_s[:, h * HS : (h + 1) * HS]
            sc = jnp.where(ok, dot(qh, keys, 1, 1), NEG)
            old = m_s[h]
            m = jnp.maximum(old, jnp.max(sc, axis=1, keepdims=True))
            alpha = jnp.exp2((old - m) * scale)
            mm = jnp.concatenate([m, m], 1)
            p = jnp.exp2((sc - mm) * scale)
            m_s[h] = m
            l_s[h] = l_s[h] * alpha + (p[:, :HS] + p[:, HS:])
            sc_s[a, h] = sc[:, :HS]
            sc_s[b, h] = sc[:, HS:]

    relay(3, 13)
    come(1, 15)
    attend(1, 15)
    attend(3, 13)
    relay(6, 10)
    come(16, 2, 4, 14, 12)
    attend(2, 16)
    attend(4, 14)
    attend(6, 12)
    come(5)
    attend(5, 10)
    come(7, 11)
    attend(7, 11)
    come(8, 9)
    attend(8, 9)
    decay_products()
    for h in range(HEADS):
        m = m_s[h]
        inv = 1.0 / jnp.sum(l_s[h], axis=1, keepdims=True)
        mixed = jnp.zeros((ROWS, HS), F32)
        for a in range(0, REACH, 2):
            parts = [(jnp.exp2((sc_s[k, h] - m) * scale) * inv).astype(BF) for k in (a, a + 1)]
            mixed = mixed + dot(jnp.concatenate(parts, 1), v_s[a : a + 2].reshape(2 * ROWS, HS))
        last = (jnp.exp2((sc_s[REACH, h] - m) * scale) * inv).astype(BF)
        mixed = mixed + dot(last, v_s[REACH])
        x_s[:, h * HS : (h + 1) * HS] = mixed.astype(BF)

    loads[5].wait()
    loads[6].wait()

    def kv_done():
        for i in range(2):
            for b in FIRST:
                hop(i, 0, b).wait_send()
            for a, bs in RELAY.items():
                for b in bs:
                    hop(i, a, b).wait_send()

    def pass_done(p):
        pair_copy(p).wait_send()
        share_copy(p, core).wait_send()
        all_out(rs_s.at[p, pl.ds(0, NY - 1)], rs_ss.at[p])
        for q in (2 * p, 2 * p + 1):
            all_out(e1_s.at[q, pl.ds(0, NZ - 1)], e1_ss.at[q])
            all_out(t_s.at[q, pl.ds(0, NX - 1)], t_ss.at[q])
            all_out(st_s.at[q, pl.ds(0, NZ - 1)], e3_ss.at[q])

    lane_half = lax.broadcasted_iota(jnp.int32, (HALF, 128), 1)

    def e1_copy(q, to, slot):
        o, dev = to
        return remote(cb_s.at[q, o], e1_s.at[q, slot], e1_ss.at[q], e1_rs.at[q], dev)

    def t_copy(q, to, slot):
        o, dev = to
        return remote(tsrc_s.at[q], t_s.at[q, slot], t_ss.at[q], t_rs.at[q], dev)

    def e3_copy(q, to, slot):
        o, dev = to
        return remote(e3src_s.at[q, o], st_s.at[q, slot], e3_ss.at[q], e3_rs.at[q], dev)

    def pair_copy(p):
        return remote(pay_s.at[p, 1 - core], pr_s.at[p], pair_ss.at[p], pair_rs.at[p], partner)

    def y_copy(p, o, dev, slot):
        return remote(ysrc_s.at[p], rs_s.at[p, slot], rs_ss.at[p], rs_rs.at[p], dev)

    def share_copy(p, half):
        return remote(ag_s.at[p, half], ag_s.at[p, half], ag_ss.at[p], ag_rs.at[p], partner)


    for p in range(2):
        if p == 0:
            xb = x_s[...]
            xf = xb.astype(F32)
            s1 = s2 = jnp.sum(xf * xf, axis=1, keepdims=True)
        else:
            gv = gated_s[...]
            s1 = jnp.sum(gv * gv, axis=1, keepdims=True)
            gg = gv * gain_s[...]
            s2 = jnp.sum(gg * gg, axis=1, keepdims=True)
            xb = gg.astype(BF)
        partial = jnp.concatenate([dot(xb, w_s[...]), pack4(s1, s2, col)], 1)
        pay_s[p] = partial.reshape(2, HALF, 384)
        pair = pair_copy(p)
        pair.start()
        pair.wait_recv()
        both = pay_s[p, core] + pr_s[p]
        q1, q2 = unpack4(both[:, 256:])
        mine = jnp.concatenate([both[:, :256], pack4(q1, q2, lane_half)], 1).astype(BF)
        ysrc_s[p] = mine
        rs_s[p, chip] = mine
        each(NY, lambda j, p=p: y_copy(p, ypeer(j)[0], ypeer(j)[1], chip).start())
        all_in(rs_s.at[p, pl.ds(0, NY - 1)], rs_rs.at[p])
        tot = jnp.sum(rs_s[p].astype(F32), axis=0)
        q1, q2 = unpack4(tot[:, 256:])
        if p == 0:
            scale1 = jnp.ones_like(q1)
        else:
            scale1 = jnp.sqrt(q1 * (1.0 / CHANNELS) + EPS)
        spread = jnp.sqrt(q2 / (scale1 * scale1) * (1.0 / CHANNELS) + EPS)
        proj = tot[:, :256] / (scale1 * spread)
        ag_s[p, core] = jnp.concatenate([proj, pack4(scale1, spread, lane_half)], 1).astype(BF)
        share_copy(p, core).start()
        share_copy(p, 1 - core).wait_recv()
        agv = ag_s[p].reshape(ROWS, 384)
        b_in = agv[:, :128]
        c_out = agv[:, 128:256]
        scale1, spread = unpack4(agv[:, 256:].astype(F32))
        if p == 1:
            f1 = gated_s[...] * (1.0 / scale1) * gain_s[...]
            out1[...] = f1
            xf = f1.astype(BF).astype(F32)
        xn = (xf * (1.0 / spread)).astype(BF)

        b_wide = jnp.transpose(b_in.astype(F32))
        b_rows = b_wide.astype(BF)
        for half in range(2):
            for hp in (2 * half, 2 * half + 1):
                xp = xn[:, hp * 128 : hp * 128 + 128]
                one, two = [
                    dot((b_wide * tail_s[h : h + 1, :]).astype(BF), xp) for h in (2 * hp, 2 * hp + 1)
                ]
                contrib = jnp.where(col < 64, one, two).astype(BF)
                for nq in range(8):
                    cb_s[2 * p + half, 8 * (hp % 2) + nq] = contrib[nq * SLICE : (nq + 1) * SLICE]
            each(NZ, lambda j, q=2 * p + half: e1_copy(q, zpeer(j), z).start())
            e1_s[2 * p + half, z] = cb_s[2 * p + half, z]

        gram = dot(c_out, b_rows)
        for hp in range(PAIRS):
            cs = slice(hp * 128, hp * 128 + 128)
            mix = jnp.concatenate([gram * decay_s[2 * hp], gram * decay_s[2 * hp + 1]], 1).astype(BF)
            xp = xn[:, cs]
            zero = jnp.zeros_like(xp)
            both = jnp.concatenate([jnp.where(col < 64, xp, zero), jnp.where(col < 64, zero, xp)], 0)
            y_s[:, cs] = dot(mix, both)

        if p == 0:
            kv_done()
            all_out(dz_s.at[pl.ds(0, NZ - 1)], d_ss)
        else:
            pass_done(0)
        for half in range(2):
            q = 2 * p + half
            all_in(e1_s.at[q, pl.ds(0, NZ - 1)], e1_rs.at[q])
            state = jnp.zeros((SLICE, 128), F32)
            for zz in range(NZ):
                pre_s[half, zz] = state
                state = dz_s[zz, half : half + 1, :] * state + e1_s[q, zz].astype(F32)
            tsrc_s[q, :SLICE] = state
            t_s[q, x] = tsrc_s[q]
            each(NX, lambda j, q=q: t_copy(q, xpeer(j), x).start())
        for half in range(2):
            q = 2 * p + half
            all_in(t_s.at[q, pl.ds(0, NX - 1)], t_rs.at[q])
            before = jnp.zeros((SLICE, 128), F32)
            for xx in range(NX - 1):
                decay = t_s[q, xx, SLICE : SLICE + 1]
                before = jnp.where(xx < x, decay * before + t_s[q, xx, :SLICE], before)
            for zz in range(NZ):
                e3src_s[q, zz] = (pre_s[half, zz] + dp_s[zz, half : half + 1, :] * before).astype(BF)
            each(NZ, lambda j, q=q: e3_copy(q, zpeer(j), z).start())
            st_s[q, z] = e3src_s[q, z]
        for half in range(2):
            q = 2 * p + half
            all_in(st_s.at[q, pl.ds(0, NZ - 1)], e3_rs.at[q])
            for hp in (2 * half, 2 * half + 1):
                cs = slice(hp * 128, hp * 128 + 128)
                st = st_s[q, 8 * (hp % 2) : 8 * (hp % 2) + 8].reshape(128, 128)
                y = y_s[:, cs] + dot(c_out, st) * expell_s[:, cs]
                gated_s[:, cs] = y * silu_s[:, cs]

    gv = gated_s[...]
    hi, lo = split(gv * gv)
    ones8 = jnp.ones((8, COLS), BF)
    mine = dot(ones8, hi.astype(BF), 1, 1) + dot(ones8, lo.astype(BF), 1, 1)
    gsrc_s[...] = mine
    g_s[t] = mine

    def g_send(j):
        o, dev = tpeer(j)
        remote(gsrc_s, g_s.at[t], g_ss, g_rs, dev).start()

    each(NT, g_send)
    pass_done(1)
    all_in(g_s.at[pl.ds(0, NT - 1)], g_rs)
    total = jnp.sum(g_s[...], axis=0)[0:1, :]
    inv = lax.rsqrt(total * (1.0 / CHANNELS) + EPS)
    inv = jnp.transpose(jnp.broadcast_to(inv, (128, 128)))
    for hp in range(PAIRS):
        cs = slice(hp * 128, hp * 128 + 128)
        out2[:, cs] = gated_s[:, cs] * inv * gain_s[:, cs]
    all_out(g_s.at[pl.ds(0, NT - 1)], g_ss)


def on_device(
    queries, rotated_keys, values, decay_rates, decay_codes, gate_input, norm_gain, bc_weight
):
    vm = pltpu.VMEM
    dma = pltpu.SemaphoreType.DMA
    anyspace = pl.BlockSpec(memory_space=pl.ANY)
    block = vm((ROWS, COLS), F32)
    scratch = [
        vm((ROWS, COLS), BF),
        vm((REACH + 1, ROWS, HS), BF),
        vm((REACH + 1, ROWS, HS), BF),
        vm((NH, ROWS), jnp.int32),
        vm((ROWS, COLS), BF),
        vm((1, COLS), F32),
        vm((COLS, 256), BF),
        vm((REACH + 1, HEADS, ROWS, HS), F32),
        vm((HEADS, ROWS, HS), F32),
        vm((HEADS, ROWS, HS), F32),
        vm((NH, ROWS, ROWS), F32),
        vm((NH, ROWS), F32),
        vm((ROWS, COLS), F32),
        vm((ROWS, COLS), F32),
        vm((2, 2, 128), F32),
        vm((NZ, 2, 128), F32),
        vm((NZ, 2, 128), F32),
        vm((ROWS, COLS), BF),
        vm((ROWS, COLS), F32),
        vm((ROWS, COLS), F32),
        vm((2, 2, HALF, 384), F32),
        vm((2, HALF, 384), F32),
        vm((2, HALF, 384), BF),
        vm((2, NY, HALF, 384), BF),
        vm((2, 2, HALF, 384), BF),
        vm((4, NZ, SLICE, 128), BF),
        vm((4, NZ, SLICE, 128), BF),
        vm((2, NZ, SLICE, 128), F32),
        vm((4, SLICE + 8, 128), F32),
        vm((4, NX, SLICE + 8, 128), F32),
        vm((4, NZ, SLICE, 128), BF),
        vm((4, NZ, SLICE, 128), BF),
        vm((8, 128), F32),
        vm((NT, 8, 128), F32),
        dma((7,)),
        dma((2, REACH + 1)), dma((2, REACH + 1)),
        dma, dma,
        dma((2,)), dma((2,)), dma((2,)), dma((2,)), dma((2,)), dma((2,)),
        dma((4,)), dma((4,)), dma((4,)), dma((4,)), dma((4,)), dma((4,)),
        dma, dma,
    ]
    return pl.pallas_call(
        kernel,
        out_shape=(block, block),
        in_specs=[anyspace] * 3 + [pl.BlockSpec(memory_space=pltpu.SMEM)] + [anyspace] * 4,
        out_specs=(pl.BlockSpec(memory_space=vm),) * 2,
        scratch_shapes=scratch,
        compiler_params=pltpu.CompilerParams(
            collective_id=0, has_side_effects=True, vmem_limit_bytes=60 << 20
        ),
    )(queries, rotated_keys, values, decay_rates, decay_codes.T, gate_input, norm_gain, bc_weight)


def solution(mesh):
    return jax.shard_map(
        on_device,
        mesh=mesh,
        in_specs=(
            P("seq", "tp"),
            P("seq", "tp"),
            P("seq", "tp"),
            P("tp"),
            P("seq", "tp"),
            P("seq", "tp"),
            P("tp"),
            P("tp", None),
        ),
        out_specs=(P("seq", "tp"), P("seq", "tp")),
        check_vma=False,
    )
```

```python
import functools
import math

import jax
import jax.numpy as jnp
from jax import lax
from jax.experimental import pallas as pl
from jax.experimental.pallas import tpu as pltpu
from jax.sharding import PartitionSpec as P

HEADS = 4
HS = 128
NH = 8
PAIRS = NH // 2
ROWS = 128
REACH = 16
NZ = 16
NX = 4
NT = 8
NY = 4
HALF = 64
CHANNELS = 4096
COLS = 512
NS = 128
EPS = 1e-5
SLICE = 16
BF = jnp.bfloat16
F32 = jnp.float32
MESH = pl.DeviceIdType.MESH
NEG = -1e30
FIRST = (3, 13, 1, 15, 16)
RELAY = {3: (6, 4, 2), 13: (10, 14, 12), 6: (8, 7, 5), 10: (9, 11)}
NEAR = (1, 2, 3, 13, 15)


def dot(a, b, ca=1, cb=0):
    return lax.dot_general(a, b, (((ca,), (cb,)), ((), ())), preferred_element_type=F32)


def split(a):
    hi = a.astype(BF).astype(F32)
    return hi, a - hi


def pack4(a, b, lane):
    ah, al = split(a)
    bh, bl = split(b)
    return jnp.where(lane < 64, jnp.where(lane < 32, ah, al), jnp.where(lane < 96, bh, bl))


def unpack4(v):
    return v[:, 0:1] + v[:, 32:33], v[:, 64:65] + v[:, 96:97]


def kernel(
    q_hbm, k_hbm, v_hbm, rates, codes_hbm, gate_hbm, gain_hbm, w_hbm,
    out1, out2,
    q_s, k_s, v_s, codes_s, gate_s, gain_s, w_s,
    sc_s, m_s, l_s, decay_s, tail_s, expell_s, silu_s,
    dexp_s, dz_s, dp_s,
    x_s, gated_s, y_s,
    pay_s, pr_s, ysrc_s, rs_s, ag_s, csrc_s, cs_s, agc_s,
    cb_s, e1_s, pre_s, tsrc_s, t_s, e3src_s, st_s,
    gsrc_s, g_s,
    in_sem,
    kv_ss, kv_rs, d_ss, d_rs,
    pair_ss, pair_rs, rs_ss, rs_rs, ag_ss, ag_rs, cs_ss, cs_rs, agc_ss, agc_rs,
    e1_ss, e1_rs, t_ss, t_rs, e3_ss, e3_rs,
    g_ss, g_rs,
):
    s = lax.axis_index("seq")
    t = lax.axis_index("tp")
    x = lax.div(s, NZ)
    z = lax.rem(s, NZ)
    chip = lax.div(t, 2)
    core = lax.rem(t, 2)
    partner = (s, t + 1 - 2 * core)

    def zpeer(j):
        o = lax.rem(z + j, NZ)
        return o, (x * NZ + o, t)

    def xpeer(j):
        o = lax.rem(x + j, NX)
        return o, (o * NZ + z, t)

    def tpeer(j):
        o = lax.rem(t + j, NT)
        return o, (s, o)

    def ypeer(j):
        o = lax.rem(chip + j, NY)
        return o, (s, 2 * o + core)

    def remote(src, dst, ss, rs, dev):
        return pltpu.make_async_remote_copy(
            src_ref=src, dst_ref=dst, send_sem=ss, recv_sem=rs, device_id=dev, device_id_type=MESH
        )

    def all_in(ref, sem):
        remote(ref, ref, sem, sem, partner).wait_recv()

    def all_out(ref, sem):
        remote(ref, ref, sem, sem, partner).wait_send()

    def along_z(body):
        body(NZ // 2)

        def step(j, c):
            body(NZ // 2 - j)
            body(NZ // 2 + j)
            return c

        lax.fori_loop(1, NZ // 2, step, 0)

    def each(n, body):
        def step(j, c):
            body(j)
            return c

        lax.fori_loop(1, n, step, 0)

    barrier = pltpu.get_barrier_semaphore()

    def greet(dev):
        pl.semaphore_signal(barrier, inc=1, device_id=dev, device_id_type=MESH)

    def block_device(k):
        return (lax.rem(s + (k + NX * NZ), NX * NZ), t)

    along_z(lambda j: greet(zpeer(j)[1]))
    for k in NEAR:
        greet(block_device(k))
        greet(block_device(-k))
    each(NX, lambda j: greet(xpeer(j)[1]))
    each(NT, lambda j: greet(tpeer(j)[1]))

    loads = [
        pltpu.make_async_copy(src, dst, in_sem.at[i])
        for i, (src, dst) in enumerate(
            (
                (k_hbm, k_s.at[0]),
                (v_hbm, v_s.at[0]),
                (codes_hbm, codes_s),
                (q_hbm, q_s),
                (gate_hbm, gate_s),
                (gain_hbm, gain_s.at[0]),
                (w_hbm, w_s),
            )
        )
    ]
    for c in loads:
        c.start()

    pl.semaphore_wait(barrier, 2 * len(NEAR) + (NX - 1) + (NZ - 1) + (NT - 1))

    def hop(i, a, b):
        buf = (k_s, v_s)[i]
        return remote(buf.at[a], buf.at[b], kv_ss.at[i, b], kv_rs.at[i, b], block_device(b - a))

    def arrived(i, b):
        hop(i, b - 1, b).wait_recv()

    loads[0].wait()
    loads[1].wait()
    for group in (FIRST[:2], FIRST[2:]):
        for i in range(2):
            for b in group:
                hop(i, 0, b).start()

    row = lax.broadcasted_iota(jnp.int32, (ROWS, ROWS), 0)
    col = lax.broadcasted_iota(jnp.int32, (ROWS, ROWS), 1)
    lane1 = lax.broadcasted_iota(jnp.int32, (1, 128), 1)
    lower = row >= col
    upper = jnp.where(row <= col, 1.0, 0.0).astype(BF)
    loads[2].wait()
    codes = codes_s[...]
    code_hi = lax.shift_right_logical(codes, 7).astype(F32).astype(BF)
    code_lo = (codes & 127).astype(F32).astype(BF)
    cum_rows = dot(code_hi, upper) * 128.0 + dot(code_lo, upper)
    cum = jnp.transpose(jnp.concatenate([cum_rows, jnp.zeros((128 - NH, ROWS), F32)], 0))
    for hp in range(PAIRS):
        ells, ends = [], []
        for h in (2 * hp, 2 * hp + 1):
            rate = -rates[h]
            ell = cum[:, h : h + 1] * rate
            ell_row = cum_rows[h : h + 1, :] * rate
            end = ell[ROWS - 1 :, :]
            gap = jnp.where(lower, ell - ell_row, 0.0)
            decay_s[h] = jnp.where(lower, jnp.exp(gap), 0.0)
            tail_s[h : h + 1, :] = jnp.exp(end - ell_row)
            ells.append(jnp.exp(ell))
            ends.append(jnp.exp(end))
        cs = slice(hp * 128, hp * 128 + 128)
        expell_s[:, cs] = jnp.where(col < 64, ells[0], ells[1])
        dexp_s[hp % 2, hp // 2 : hp // 2 + 1, :] = jnp.where(lane1 < 64, ends[0], ends[1])

    def d_send(j):
        o, dev = zpeer(j)
        remote(dexp_s.at[lax.div(o, 8)], dz_s.at[z], d_ss, d_rs, dev).start()

    along_z(d_send)
    dz_s[z] = dexp_s[lax.div(z, 8)]

    loads[3].wait()
    scale = math.log2(math.e) / math.sqrt(HS)
    diff = col - row
    own_k = k_s[0]
    for h in range(HEADS):
        qh = q_s[:, h * HS : (h + 1) * HS]
        sc = jnp.where(lower, dot(qh, own_k, 1, 1), NEG)
        m = jnp.max(sc, axis=1, keepdims=True)
        m_s[h] = jnp.broadcast_to(m, (ROWS, HS))
        l_s[h] = jnp.exp2((sc - m) * scale)
        sc_s[0, h] = sc

    loads[4].wait()
    g = gate_s[...].astype(F32)
    silu_s[...] = g / (1.0 + jnp.exp(-g))

    def decay_products():
        all_in(dz_s.at[pl.ds(0, NZ - 1)], d_rs)
        running = jnp.ones((2, 128), F32)
        for zz in range(NZ):
            dp_s[zz] = running
            running = running * dz_s[zz]
        for p in range(2):
            for half in range(2):
                tsrc_s[2 * p + half, SLICE:] = jnp.broadcast_to(running[half : half + 1], (8, 128))

    def relay(a, b):
        for i in range(2):
            for k in (a, b):
                arrived(i, k)
                hop(i, k, RELAY[k][0]).start()
        for n in (1, 2):
            for k in (a, b):
                for i in range(2):
                    for to in RELAY[k][n : n + 1]:
                        hop(i, k, to).start()

    def come(*slots):
        for b in slots:
            arrived(0, b)
            arrived(1, b)

    def attend(a, b):
        big = jnp.int32(1 << 20)

        def limit(k):
            return jnp.where(s >= k, jnp.int32((k - REACH) * ROWS), big)

        keys = jnp.concatenate([k_s[a], k_s[b]], 0)
        ok = jnp.concatenate([diff > limit(a), diff > limit(b)], 1)
        for h in range(HEADS):
            qh = q_s[:, h * HS : (h + 1) * HS]
            sc = jnp.where(ok, dot(qh, keys, 1, 1), NEG)
            old = m_s[h]
            m = jnp.maximum(old, jnp.max(sc, axis=1, keepdims=True))
            alpha = jnp.exp2((old - m) * scale)
            mm = jnp.concatenate([m, m], 1)
            p = jnp.exp2((sc - mm) * scale)
            m_s[h] = m
            l_s[h] = l_s[h] * alpha + (p[:, :HS] + p[:, HS:])
            sc_s[a, h] = sc[:, :HS]
            sc_s[b, h] = sc[:, HS:]

    relay(3, 13)
    come(1, 15)
    attend(1, 15)
    attend(3, 13)
    relay(6, 10)
    come(16, 2, 4, 14, 12)
    attend(2, 16)
    attend(4, 14)
    attend(6, 12)
    come(5)
    attend(5, 10)
    come(7, 11)
    attend(7, 11)
    come(8, 9)
    attend(8, 9)
    decay_products()
    for h in range(HEADS):
        m = m_s[h]
        inv = 1.0 / jnp.sum(l_s[h], axis=1, keepdims=True)
        mixed = jnp.zeros((ROWS, HS), F32)
        for a in range(0, REACH, 2):
            parts = [(jnp.exp2((sc_s[k, h] - m) * scale) * inv).astype(BF) for k in (a, a + 1)]
            mixed = mixed + dot(jnp.concatenate(parts, 1), v_s[a : a + 2].reshape(2 * ROWS, HS))
        last = (jnp.exp2((sc_s[REACH, h] - m) * scale) * inv).astype(BF)
        mixed = mixed + dot(last, v_s[REACH])
        x_s[:, h * HS : (h + 1) * HS] = mixed.astype(BF)

    loads[5].wait()
    loads[6].wait()

    def kv_done():
        for i in range(2):
            for b in FIRST:
                hop(i, 0, b).wait_send()
            for a, bs in RELAY.items():
                for b in bs:
                    hop(i, a, b).wait_send()

    def pass_done(p):
        pair_copy(p).wait_send()
        share_copy(p, core).wait_send()
        share_c(p, core).wait_send()
        all_out(cs_s.at[p, pl.ds(0, NY - 1)], cs_ss.at[p])
        all_out(rs_s.at[p, pl.ds(0, NY - 1)], rs_ss.at[p])
        for q in (2 * p, 2 * p + 1):
            all_out(e1_s.at[q, pl.ds(0, NZ - 1)], e1_ss.at[q])
            all_out(t_s.at[q, pl.ds(0, NX - 1)], t_ss.at[q])
            all_out(st_s.at[q, pl.ds(0, NZ - 1)], e3_ss.at[q])

    lane_half = lax.broadcasted_iota(jnp.int32, (HALF, 128), 1)

    def e1_copy(q, to, slot):
        o, dev = to
        return remote(cb_s.at[q, o], e1_s.at[q, slot], e1_ss.at[q], e1_rs.at[q], dev)

    def t_copy(q, to, slot):
        o, dev = to
        return remote(tsrc_s.at[q], t_s.at[q, slot], t_ss.at[q], t_rs.at[q], dev)

    def e3_copy(q, to, slot):
        o, dev = to
        return remote(e3src_s.at[q, o], st_s.at[q, slot], e3_ss.at[q], e3_rs.at[q], dev)

    def pair_copy(p):
        return remote(pay_s.at[p, 1 - core], pr_s.at[p], pair_ss.at[p], pair_rs.at[p], partner)

    def y_copy(p, o, dev, slot):
        return remote(ysrc_s.at[p], rs_s.at[p, slot], rs_ss.at[p], rs_rs.at[p], dev)

    def c_copy(p, dev):
        return remote(csrc_s.at[p], cs_s.at[p, chip], cs_ss.at[p], cs_rs.at[p], dev)

    def share_c(p, half):
        return remote(agc_s.at[p, half], agc_s.at[p, half], agc_ss.at[p], agc_rs.at[p], partner)

    def share_copy(p, half):
        return remote(ag_s.at[p, half], ag_s.at[p, half], ag_ss.at[p], ag_rs.at[p], partner)


    for p in range(2):
        if p == 0:
            xb = x_s[...]
            xf = xb.astype(F32)
            s1 = s2 = jnp.sum(xf * xf, axis=1, keepdims=True)
        else:
            gv = gated_s[...]
            s1 = jnp.sum(gv * gv, axis=1, keepdims=True)
            gg = gv * gain_s[...]
            s2 = jnp.sum(gg * gg, axis=1, keepdims=True)
            xb = gg.astype(BF)
        partial = jnp.concatenate([dot(xb, w_s[...]), pack4(s1, s2, col)], 1)
        pay_s[p] = partial.reshape(2, HALF, 384)
        pair = pair_copy(p)
        pair.start()
        pair.wait_recv()
        both = pay_s[p, core] + pr_s[p]
        q1, q2 = unpack4(both[:, 256:])
        mine = jnp.concatenate([both[:, :128], pack4(q1, q2, lane_half)], 1).astype(BF)
        ysrc_s[p] = mine
        rs_s[p, chip] = mine
        each(NY, lambda j, p=p: y_copy(p, ypeer(j)[0], ypeer(j)[1], chip).start())
        csrc_s[p] = both[:, 128:256]
        cs_s[p, chip] = both[:, 128:256]
        each(NY, lambda j, p=p: c_copy(p, ypeer(j)[1]).start())
        all_in(rs_s.at[p, pl.ds(0, NY - 1)], rs_rs.at[p])
        tot = jnp.sum(rs_s[p].astype(F32), axis=0)
        q1, q2 = unpack4(tot[:, 128:])
        if p == 0:
            scale1 = jnp.ones_like(q1)
        else:
            scale1 = jnp.sqrt(q1 * (1.0 / CHANNELS) + EPS)
        spread = jnp.sqrt(q2 / (scale1 * scale1) * (1.0 / CHANNELS) + EPS)
        per_row = 1.0 / (scale1 * spread)
        proj = tot[:, :128] * per_row
        ag_s[p, core] = jnp.concatenate([proj, pack4(scale1, spread, lane_half)], 1).astype(BF)
        share_copy(p, core).start()
        share_copy(p, 1 - core).wait_recv()
        agv = ag_s[p].reshape(ROWS, 256)
        b_in = agv[:, :128]
        scale1, spread = unpack4(agv[:, 128:].astype(F32))
        if p == 1:
            f1 = gated_s[...] * (1.0 / scale1) * gain_s[...]
            out1[...] = f1
            xf = f1.astype(BF).astype(F32)
        xn = (xf * (1.0 / spread)).astype(BF)

        b_wide = jnp.transpose(b_in.astype(F32))
        b_rows = b_wide.astype(BF)
        for half in range(2):
            for hp in (2 * half, 2 * half + 1):
                xp = xn[:, hp * 128 : hp * 128 + 128]
                one, two = [
                    dot((b_wide * tail_s[h : h + 1, :]).astype(BF), xp) for h in (2 * hp, 2 * hp + 1)
                ]
                contrib = jnp.where(col < 64, one, two).astype(BF)
                for nq in range(8):
                    cb_s[2 * p + half, 8 * (hp % 2) + nq] = contrib[nq * SLICE : (nq + 1) * SLICE]
            along_z(lambda j, q=2 * p + half: e1_copy(q, zpeer(j), z).start())
            e1_s[2 * p + half, z] = cb_s[2 * p + half, z]

        all_in(cs_s.at[p, pl.ds(0, NY - 1)], cs_rs.at[p])
        agc_s[p, core] = (jnp.sum(cs_s[p], axis=0) * per_row).astype(BF)
        share_c(p, core).start()
        share_c(p, 1 - core).wait_recv()
        c_out = agc_s[p].reshape(ROWS, NS)
        gram = dot(c_out, b_rows)
        for hp in range(PAIRS):
            cs = slice(hp * 128, hp * 128 + 128)
            mix = jnp.concatenate([gram * decay_s[2 * hp], gram * decay_s[2 * hp + 1]], 1).astype(BF)
            xp = xn[:, cs]
            zero = jnp.zeros_like(xp)
            both = jnp.concatenate([jnp.where(col < 64, xp, zero), jnp.where(col < 64, zero, xp)], 0)
            y_s[:, cs] = dot(mix, both)

        if p == 0:
            kv_done()
            all_out(dz_s.at[pl.ds(0, NZ - 1)], d_ss)
        else:
            pass_done(0)
        for half in range(2):
            q = 2 * p + half
            all_in(e1_s.at[q, pl.ds(0, NZ - 1)], e1_rs.at[q])
            state = jnp.zeros((SLICE, 128), F32)
            for zz in range(NZ):
                pre_s[half, zz] = state
                state = dz_s[zz, half : half + 1, :] * state + e1_s[q, zz].astype(F32)
            tsrc_s[q, :SLICE] = state
            t_s[q, x] = tsrc_s[q]
            each(NX, lambda j, q=q: t_copy(q, xpeer(j), x).start())
        for half in range(2):
            q = 2 * p + half
            all_in(t_s.at[q, pl.ds(0, NX - 1)], t_rs.at[q])
            before = jnp.zeros((SLICE, 128), F32)
            for xx in range(NX - 1):
                decay = t_s[q, xx, SLICE : SLICE + 1]
                before = jnp.where(xx < x, decay * before + t_s[q, xx, :SLICE], before)
            for zz in range(NZ):
                e3src_s[q, zz] = (pre_s[half, zz] + dp_s[zz, half : half + 1, :] * before).astype(BF)
            along_z(lambda j, q=q: e3_copy(q, zpeer(j), z).start())
            st_s[q, z] = e3src_s[q, z]
        for half in range(2):
            q = 2 * p + half
            all_in(st_s.at[q, pl.ds(0, NZ - 1)], e3_rs.at[q])
            for hp in (2 * half, 2 * half + 1):
                cs = slice(hp * 128, hp * 128 + 128)
                st = st_s[q, 8 * (hp % 2) : 8 * (hp % 2) + 8].reshape(128, 128)
                y = y_s[:, cs] + dot(c_out, st) * expell_s[:, cs]
                gated_s[:, cs] = y * silu_s[:, cs]

    gv = gated_s[...]
    hi, lo = split(gv * gv)
    ones8 = jnp.ones((8, COLS), BF)
    mine = dot(ones8, hi.astype(BF), 1, 1) + dot(ones8, lo.astype(BF), 1, 1)
    gsrc_s[...] = mine
    g_s[t] = mine

    def g_send(j):
        o, dev = tpeer(j)
        remote(gsrc_s, g_s.at[t], g_ss, g_rs, dev).start()

    each(NT, g_send)
    pass_done(1)
    all_in(g_s.at[pl.ds(0, NT - 1)], g_rs)
    total = jnp.sum(g_s[...], axis=0)[0:1, :]
    inv = lax.rsqrt(total * (1.0 / CHANNELS) + EPS)
    inv = jnp.transpose(jnp.broadcast_to(inv, (128, 128)))
    for hp in range(PAIRS):
        cs = slice(hp * 128, hp * 128 + 128)
        out2[:, cs] = gated_s[:, cs] * inv * gain_s[:, cs]
    all_out(g_s.at[pl.ds(0, NT - 1)], g_ss)


def on_device(
    queries, rotated_keys, values, decay_rates, decay_codes, gate_input, norm_gain, bc_weight
):
    vm = pltpu.VMEM
    dma = pltpu.SemaphoreType.DMA
    anyspace = pl.BlockSpec(memory_space=pl.ANY)
    block = vm((ROWS, COLS), F32)
    scratch = [
        vm((ROWS, COLS), BF),
        vm((REACH + 1, ROWS, HS), BF),
        vm((REACH + 1, ROWS, HS), BF),
        vm((NH, ROWS), jnp.int32),
        vm((ROWS, COLS), BF),
        vm((1, COLS), F32),
        vm((COLS, 256), BF),
        vm((REACH + 1, HEADS, ROWS, HS), F32),
        vm((HEADS, ROWS, HS), F32),
        vm((HEADS, ROWS, HS), F32),
        vm((NH, ROWS, ROWS), F32),
        vm((NH, ROWS), F32),
        vm((ROWS, COLS), F32),
        vm((ROWS, COLS), F32),
        vm((2, 2, 128), F32),
        vm((NZ, 2, 128), F32),
        vm((NZ, 2, 128), F32),
        vm((ROWS, COLS), BF),
        vm((ROWS, COLS), F32),
        vm((ROWS, COLS), F32),
        vm((2, 2, HALF, 384), F32),
        vm((2, HALF, 384), F32),
        vm((2, HALF, 256), BF),
        vm((2, NY, HALF, 256), BF),
        vm((2, 2, HALF, 256), BF),
        vm((2, HALF, 128), F32),
        vm((2, NY, HALF, 128), F32),
        vm((2, 2, HALF, 128), BF),
        vm((4, NZ, SLICE, 128), BF),
        vm((4, NZ, SLICE, 128), BF),
        vm((2, NZ, SLICE, 128), F32),
        vm((4, SLICE + 8, 128), F32),
        vm((4, NX, SLICE + 8, 128), F32),
        vm((4, NZ, SLICE, 128), BF),
        vm((4, NZ, SLICE, 128), BF),
        vm((8, 128), F32),
        vm((NT, 8, 128), F32),
        dma((7,)),
        dma((2, REACH + 1)), dma((2, REACH + 1)),
        dma, dma,
        dma((2,)), dma((2,)), dma((2,)), dma((2,)), dma((2,)), dma((2,)),
        dma((2,)), dma((2,)), dma((2,)), dma((2,)),
        dma((4,)), dma((4,)), dma((4,)), dma((4,)), dma((4,)), dma((4,)),
        dma, dma,
    ]
    return pl.pallas_call(
        kernel,
        out_shape=(block, block),
        in_specs=[anyspace] * 3 + [pl.BlockSpec(memory_space=pltpu.SMEM)] + [anyspace] * 4,
        out_specs=(pl.BlockSpec(memory_space=vm),) * 2,
        scratch_shapes=scratch,
        compiler_params=pltpu.CompilerParams(
            collective_id=0, has_side_effects=True, vmem_limit_bytes=60 << 20
        ),
    )(queries, rotated_keys, values, decay_rates, decay_codes.T, gate_input, norm_gain, bc_weight)


def solution(mesh):
    return jax.shard_map(
        on_device,
        mesh=mesh,
        in_specs=(
            P("seq", "tp"),
            P("seq", "tp"),
            P("seq", "tp"),
            P("tp"),
            P("seq", "tp"),
            P("seq", "tp"),
            P("tp"),
            P("tp", None),
        ),
        out_specs=(P("seq", "tp"), P("seq", "tp")),
        check_vma=False,
    )
```

```python
import functools
import math

import jax
import jax.numpy as jnp
from jax import lax
from jax.experimental import pallas as pl
from jax.experimental.pallas import tpu as pltpu
from jax.sharding import PartitionSpec as P

HEADS = 4
HS = 128
NH = 8
PAIRS = NH // 2
ROWS = 128
REACH = 16
NZ = 16
NX = 4
NT = 8
NY = 4
HALF = 64
CHANNELS = 4096
COLS = 512
NS = 128
EPS = 1e-5
SLICE = 16
BF = jnp.bfloat16
F32 = jnp.float32
MESH = pl.DeviceIdType.MESH
NEG = -1e30
FIRST = (3, 13, 1, 15, 16)
RELAY = {3: (6, 4, 2), 13: (10, 14, 12), 6: (8, 7, 5), 10: (9, 11)}
NEAR = (1, 2, 3, 13, 15)


def dot(a, b, ca=1, cb=0):
    return lax.dot_general(a, b, (((ca,), (cb,)), ((), ())), preferred_element_type=F32)


def split(a):
    hi = a.astype(BF).astype(F32)
    return hi, a - hi


def pack4(a, b, lane):
    ah, al = split(a)
    bh, bl = split(b)
    return jnp.where(lane < 64, jnp.where(lane < 32, ah, al), jnp.where(lane < 96, bh, bl))


def unpack4(v):
    return v[:, 0:1] + v[:, 32:33], v[:, 64:65] + v[:, 96:97]


def kernel(
    q_hbm, k_hbm, v_hbm, rates_hbm, codes_hbm, gate_hbm, gain_hbm, w_hbm,
    out1, out2,
    rates, q_s, k_s, v_s, codes_s, gate_s, gain_s, w_s,
    sc_s, m_s, l_s, decay_s, tail_s, expell_s, silu_s,
    dexp_s, dz_s, dp_s,
    x_s, gated_s, y_s,
    pay_s, pr_s, ysrc_s, rs_s, ag_s, csrc_s, cs_s, agc_s,
    cb_s, e1_s, pre_s, tsrc_s, t_s, e3src_s, st_s,
    gsrc_s, g_s,
    in_sem,
    kv_ss, kv_rs, d_ss, d_rs,
    pair_ss, pair_rs, rs_ss, rs_rs, ag_ss, ag_rs, cs_ss, cs_rs, agc_ss, agc_rs,
    e1_ss, e1_rs, t_ss, t_rs, e3_ss, e3_rs,
    g_ss, g_rs,
):
    s = lax.axis_index("seq")
    t = lax.axis_index("tp")
    x = lax.div(s, NZ)
    z = lax.rem(s, NZ)
    chip = lax.div(t, 2)
    core = lax.rem(t, 2)
    partner = (s, t + 1 - 2 * core)

    def zpeer(j):
        o = lax.rem(z + j, NZ)
        return o, (x * NZ + o, t)

    def xpeer(j):
        o = lax.rem(x + j, NX)
        return o, (o * NZ + z, t)

    def tpeer(j):
        o = lax.rem(t + j, NT)
        return o, (s, o)

    def ypeer(j):
        o = lax.rem(chip + j, NY)
        return o, (s, 2 * o + core)

    def remote(src, dst, ss, rs, dev):
        return pltpu.make_async_remote_copy(
            src_ref=src, dst_ref=dst, send_sem=ss, recv_sem=rs, device_id=dev, device_id_type=MESH
        )

    def all_in(ref, sem):
        remote(ref, ref, sem, sem, partner).wait_recv()

    def all_out(ref, sem):
        remote(ref, ref, sem, sem, partner).wait_send()

    def each(n, body):
        body(n // 2)

        def step(j, c):
            body(n // 2 - j)
            body(n // 2 + j)
            return c

        lax.fori_loop(1, n // 2, step, 0)

    barrier = pltpu.get_barrier_semaphore()

    def greet(dev):
        pl.semaphore_signal(barrier, inc=1, device_id=dev, device_id_type=MESH)

    def block_device(k):
        return (lax.rem(s + (k + NX * NZ), NX * NZ), t)

    each(NZ, lambda j: greet(zpeer(j)[1]))
    for k in NEAR:
        greet(block_device(k))
        greet(block_device(-k))
    each(NX, lambda j: greet(xpeer(j)[1]))
    each(NT, lambda j: greet(tpeer(j)[1]))

    loads = [
        pltpu.make_async_copy(src, dst, in_sem.at[i])
        for i, (src, dst) in enumerate(
            (
                (k_hbm, k_s.at[0]),
                (v_hbm, v_s.at[0]),
                (codes_hbm, codes_s),
                (rates_hbm, rates),
                (q_hbm, q_s),
                (gate_hbm, gate_s),
                (gain_hbm, gain_s.at[0]),
                (w_hbm, w_s),
            )
        )
    ]
    for c in loads:
        c.start()

    pl.semaphore_wait(barrier, 2 * len(NEAR) + (NX - 1) + (NZ - 1) + (NT - 1))

    def hop(i, a, b):
        buf = (k_s, v_s)[i]
        return remote(buf.at[a], buf.at[b], kv_ss.at[i, b], kv_rs.at[i, b], block_device(b - a))

    def arrived(i, b):
        hop(i, b - 1, b).wait_recv()

    loads[0].wait()
    loads[1].wait()
    for group in (FIRST[:2], FIRST[2:]):
        for i in range(2):
            for b in group:
                hop(i, 0, b).start()

    row = lax.broadcasted_iota(jnp.int32, (ROWS, ROWS), 0)
    col = lax.broadcasted_iota(jnp.int32, (ROWS, ROWS), 1)
    lane1 = lax.broadcasted_iota(jnp.int32, (1, 128), 1)
    lower = row >= col
    upper = jnp.where(row <= col, 1.0, 0.0).astype(BF)
    loads[2].wait()
    loads[3].wait()
    codes = codes_s[...]
    code_hi = lax.shift_right_logical(codes, 7).astype(F32).astype(BF)
    code_lo = (codes & 127).astype(F32).astype(BF)
    cum_rows = dot(code_hi, upper) * 128.0 + dot(code_lo, upper)
    cum = jnp.transpose(jnp.concatenate([cum_rows, jnp.zeros((128 - NH, ROWS), F32)], 0))
    for hp in range(PAIRS):
        ells, ends = [], []
        for h in (2 * hp, 2 * hp + 1):
            rate = -rates[h]
            ell = cum[:, h : h + 1] * rate
            ell_row = cum_rows[h : h + 1, :] * rate
            end = ell[ROWS - 1 :, :]
            gap = jnp.where(lower, ell - ell_row, 0.0)
            decay_s[h] = jnp.where(lower, jnp.exp(gap), 0.0)
            tail_s[h : h + 1, :] = jnp.exp(end - ell_row)
            ells.append(jnp.exp(ell))
            ends.append(jnp.exp(end))
        cs = slice(hp * 128, hp * 128 + 128)
        expell_s[:, cs] = jnp.where(col < 64, ells[0], ells[1])
        dexp_s[hp % 2, hp // 2 : hp // 2 + 1, :] = jnp.where(lane1 < 64, ends[0], ends[1])

    def d_send(j):
        o, dev = zpeer(j)
        remote(dexp_s.at[lax.div(o, 8)], dz_s.at[z], d_ss, d_rs, dev).start()

    each(NZ, d_send)
    dz_s[z] = dexp_s[lax.div(z, 8)]

    loads[4].wait()
    scale = math.log2(math.e) / math.sqrt(HS)
    diff = col - row
    own_k = k_s[0]
    for h in range(HEADS):
        qh = q_s[:, h * HS : (h + 1) * HS]
        sc = jnp.where(lower, dot(qh, own_k, 1, 1), NEG)
        m = jnp.max(sc, axis=1, keepdims=True)
        m_s[h] = jnp.broadcast_to(m, (ROWS, HS))
        l_s[h] = jnp.exp2((sc - m) * scale)
        sc_s[0, h] = sc

    loads[5].wait()
    g = gate_s[...].astype(F32)
    silu_s[...] = g / (1.0 + jnp.exp(-g))

    def decay_products():
        all_in(dz_s.at[pl.ds(0, NZ - 1)], d_rs)
        running = jnp.ones((2, 128), F32)
        for zz in range(NZ):
            dp_s[zz] = running
            running = running * dz_s[zz]
        for p in range(2):
            for half in range(2):
                tsrc_s[2 * p + half, SLICE:] = jnp.broadcast_to(running[half : half + 1], (8, 128))

    def relay(a, b):
        for i in range(2):
            for k in (a, b):
                arrived(i, k)
                hop(i, k, RELAY[k][0]).start()
        for n in (1, 2):
            for k in (a, b):
                for i in range(2):
                    for to in RELAY[k][n : n + 1]:
                        hop(i, k, to).start()

    def come(*slots):
        for b in slots:
            arrived(0, b)
            arrived(1, b)

    def attend(a, b):
        big = jnp.int32(1 << 20)

        def limit(k):
            return jnp.where(s >= k, jnp.int32((k - REACH) * ROWS), big)

        keys = jnp.concatenate([k_s[a], k_s[b]], 0)
        ok = jnp.concatenate([diff > limit(a), diff > limit(b)], 1)
        for h in range(HEADS):
            qh = q_s[:, h * HS : (h + 1) * HS]
            sc = jnp.where(ok, dot(qh, keys, 1, 1), NEG)
            old = m_s[h]
            m = jnp.maximum(old, jnp.max(sc, axis=1, keepdims=True))
            alpha = jnp.exp2((old - m) * scale)
            mm = jnp.concatenate([m, m], 1)
            p = jnp.exp2((sc - mm) * scale)
            m_s[h] = m
            l_s[h] = l_s[h] * alpha + (p[:, :HS] + p[:, HS:])
            sc_s[a, h] = sc[:, :HS]
            sc_s[b, h] = sc[:, HS:]

    relay(3, 13)
    come(1, 15)
    attend(1, 15)
    attend(3, 13)
    relay(6, 10)
    come(16, 2, 4, 14, 12)
    attend(2, 16)
    attend(4, 14)
    attend(6, 12)
    come(5)
    attend(5, 10)
    come(7, 11)
    attend(7, 11)
    come(8, 9)
    attend(8, 9)
    decay_products()
    for h in range(HEADS):
        m = m_s[h]
        inv = 1.0 / jnp.sum(l_s[h], axis=1, keepdims=True)
        mixed = jnp.zeros((ROWS, HS), F32)
        for a in range(0, REACH, 2):
            parts = [(jnp.exp2((sc_s[k, h] - m) * scale) * inv).astype(BF) for k in (a, a + 1)]
            mixed = mixed + dot(jnp.concatenate(parts, 1), v_s[a : a + 2].reshape(2 * ROWS, HS))
        last = (jnp.exp2((sc_s[REACH, h] - m) * scale) * inv).astype(BF)
        mixed = mixed + dot(last, v_s[REACH])
        x_s[:, h * HS : (h + 1) * HS] = mixed.astype(BF)

    loads[6].wait()
    loads[7].wait()

    def kv_done():
        for i in range(2):
            for b in FIRST:
                hop(i, 0, b).wait_send()
            for a, bs in RELAY.items():
                for b in bs:
                    hop(i, a, b).wait_send()

    def pass_done(p):
        pair_copy(p).wait_send()
        share_copy(p, core).wait_send()
        share_c(p, core).wait_send()
        all_out(cs_s.at[p, pl.ds(0, NY - 1)], cs_ss.at[p])
        all_out(rs_s.at[p, pl.ds(0, NY - 1)], rs_ss.at[p])
        for q in (2 * p, 2 * p + 1):
            all_out(e1_s.at[q, pl.ds(0, NZ - 1)], e1_ss.at[q])
            all_out(t_s.at[q, pl.ds(0, NX - 1)], t_ss.at[q])
            all_out(st_s.at[q, pl.ds(0, NZ - 1)], e3_ss.at[q])

    lane_half = lax.broadcasted_iota(jnp.int32, (HALF, 128), 1)

    def e1_copy(q, to, slot):
        o, dev = to
        return remote(cb_s.at[q, o], e1_s.at[q, slot], e1_ss.at[q], e1_rs.at[q], dev)

    def t_copy(q, to, slot):
        o, dev = to
        return remote(tsrc_s.at[q], t_s.at[q, slot], t_ss.at[q], t_rs.at[q], dev)

    def e3_copy(q, to, slot):
        o, dev = to
        return remote(e3src_s.at[q, o], st_s.at[q, slot], e3_ss.at[q], e3_rs.at[q], dev)

    def pair_copy(p):
        return remote(pay_s.at[p, 1 - core], pr_s.at[p], pair_ss.at[p], pair_rs.at[p], partner)

    def y_copy(p, o, dev, slot):
        return remote(ysrc_s.at[p], rs_s.at[p, slot], rs_ss.at[p], rs_rs.at[p], dev)

    def c_copy(p, dev):
        return remote(csrc_s.at[p], cs_s.at[p, chip], cs_ss.at[p], cs_rs.at[p], dev)

    def share_c(p, half):
        return remote(agc_s.at[p, half], agc_s.at[p, half], agc_ss.at[p], agc_rs.at[p], partner)

    def share_copy(p, half):
        return remote(ag_s.at[p, half], ag_s.at[p, half], ag_ss.at[p], ag_rs.at[p], partner)


    for p in range(2):
        if p == 0:
            xb = x_s[...]
            xf = xb.astype(F32)
            s1 = s2 = jnp.sum(xf * xf, axis=1, keepdims=True)
        else:
            gv = gated_s[...]
            s1 = jnp.sum(gv * gv, axis=1, keepdims=True)
            gg = gv * gain_s[...]
            s2 = jnp.sum(gg * gg, axis=1, keepdims=True)
            xb = gg.astype(BF)
        partial = jnp.concatenate([dot(xb, w_s[...]), pack4(s1, s2, col)], 1)
        pay_s[p] = partial.reshape(2, HALF, 384)
        pair = pair_copy(p)
        pair.start()
        pair.wait_recv()
        both = pay_s[p, core] + pr_s[p]
        q1, q2 = unpack4(both[:, 256:])
        mine = jnp.concatenate([both[:, :128], pack4(q1, q2, lane_half)], 1).astype(BF)
        ysrc_s[p] = mine
        rs_s[p, chip] = mine
        each(NY, lambda j, p=p: y_copy(p, ypeer(j)[0], ypeer(j)[1], chip).start())
        csrc_s[p] = both[:, 128:256]
        cs_s[p, chip] = both[:, 128:256]
        each(NY, lambda j, p=p: c_copy(p, ypeer(j)[1]).start())
        all_in(rs_s.at[p, pl.ds(0, NY - 1)], rs_rs.at[p])
        tot = jnp.sum(rs_s[p].astype(F32), axis=0)
        q1, q2 = unpack4(tot[:, 128:])
        if p == 0:
            scale1 = jnp.ones_like(q1)
        else:
            scale1 = jnp.sqrt(q1 * (1.0 / CHANNELS) + EPS)
        spread = jnp.sqrt(q2 / (scale1 * scale1) * (1.0 / CHANNELS) + EPS)
        per_row = 1.0 / (scale1 * spread)
        proj = tot[:, :128] * per_row
        ag_s[p, core] = jnp.concatenate([proj, pack4(scale1, spread, lane_half)], 1).astype(BF)
        share_copy(p, core).start()
        share_copy(p, 1 - core).wait_recv()
        agv = ag_s[p].reshape(ROWS, 256)
        b_in = agv[:, :128]
        scale1, spread = unpack4(agv[:, 128:].astype(F32))
        if p == 1:
            f1 = gated_s[...] * (1.0 / scale1) * gain_s[...]
            out1[...] = f1
            xf = f1.astype(BF).astype(F32)
        xn = (xf * (1.0 / spread)).astype(BF)

        b_wide = jnp.transpose(b_in.astype(F32))
        b_rows = b_wide.astype(BF)
        for half in range(2):
            for hp in (2 * half, 2 * half + 1):
                xp = xn[:, hp * 128 : hp * 128 + 128]
                one, two = [
                    dot((b_wide * tail_s[h : h + 1, :]).astype(BF), xp) for h in (2 * hp, 2 * hp + 1)
                ]
                contrib = jnp.where(col < 64, one, two).astype(BF)
                for nq in range(8):
                    cb_s[2 * p + half, 8 * (hp % 2) + nq] = contrib[nq * SLICE : (nq + 1) * SLICE]
            each(NZ, lambda j, q=2 * p + half: e1_copy(q, zpeer(j), z).start())
            e1_s[2 * p + half, z] = cb_s[2 * p + half, z]

        all_in(cs_s.at[p, pl.ds(0, NY - 1)], cs_rs.at[p])
        agc_s[p, core] = (jnp.sum(cs_s[p], axis=0) * per_row).astype(BF)
        share_c(p, core).start()
        share_c(p, 1 - core).wait_recv()
        c_out = agc_s[p].reshape(ROWS, NS)
        gram = dot(c_out, b_rows)
        for hp in range(PAIRS):
            cs = slice(hp * 128, hp * 128 + 128)
            mix = jnp.concatenate([gram * decay_s[2 * hp], gram * decay_s[2 * hp + 1]], 1).astype(BF)
            xp = xn[:, cs]
            zero = jnp.zeros_like(xp)
            both = jnp.concatenate([jnp.where(col < 64, xp, zero), jnp.where(col < 64, zero, xp)], 0)
            y_s[:, cs] = dot(mix, both)

        if p == 0:
            kv_done()
            all_out(dz_s.at[pl.ds(0, NZ - 1)], d_ss)
        else:
            pass_done(0)
        for half in range(2):
            q = 2 * p + half
            all_in(e1_s.at[q, pl.ds(0, NZ - 1)], e1_rs.at[q])
            state = jnp.zeros((SLICE, 128), F32)
            for zz in range(NZ):
                pre_s[half, zz] = state
                state = dz_s[zz, half : half + 1, :] * state + e1_s[q, zz].astype(F32)
            tsrc_s[q, :SLICE] = state
            t_s[q, x] = tsrc_s[q]
            each(NX, lambda j, q=q: t_copy(q, xpeer(j), x).start())
        for half in range(2):
            q = 2 * p + half
            all_in(t_s.at[q, pl.ds(0, NX - 1)], t_rs.at[q])
            before = jnp.zeros((SLICE, 128), F32)
            for xx in range(NX - 1):
                decay = t_s[q, xx, SLICE : SLICE + 1]
                before = jnp.where(xx < x, decay * before + t_s[q, xx, :SLICE], before)
            for zz in range(NZ):
                e3src_s[q, zz] = (pre_s[half, zz] + dp_s[zz, half : half + 1, :] * before).astype(BF)
            each(NZ, lambda j, q=q: e3_copy(q, zpeer(j), z).start())
            st_s[q, z] = e3src_s[q, z]
        for half in range(2):
            q = 2 * p + half
            all_in(st_s.at[q, pl.ds(0, NZ - 1)], e3_rs.at[q])
            for hp in (2 * half, 2 * half + 1):
                cs = slice(hp * 128, hp * 128 + 128)
                st = st_s[q, 8 * (hp % 2) : 8 * (hp % 2) + 8].reshape(128, 128)
                y = y_s[:, cs] + dot(c_out, st) * expell_s[:, cs]
                gated_s[:, cs] = y * silu_s[:, cs]

    gv = gated_s[...]
    hi, lo = split(gv * gv)
    ones8 = jnp.ones((8, COLS), BF)
    mine = dot(ones8, hi.astype(BF), 1, 1) + dot(ones8, lo.astype(BF), 1, 1)
    gsrc_s[...] = mine
    g_s[t] = mine

    def g_send(j):
        o, dev = tpeer(j)
        remote(gsrc_s, g_s.at[t], g_ss, g_rs, dev).start()

    each(NT, g_send)
    pass_done(1)
    all_in(g_s.at[pl.ds(0, NT - 1)], g_rs)
    total = jnp.sum(g_s[...], axis=0)[0:1, :]
    inv = lax.rsqrt(total * (1.0 / CHANNELS) + EPS)
    inv = jnp.transpose(jnp.broadcast_to(inv, (128, 128)))
    for hp in range(PAIRS):
        cs = slice(hp * 128, hp * 128 + 128)
        out2[:, cs] = gated_s[:, cs] * inv * gain_s[:, cs]
    all_out(g_s.at[pl.ds(0, NT - 1)], g_ss)


def on_device(
    queries, rotated_keys, values, decay_rates, decay_codes, gate_input, norm_gain, bc_weight
):
    vm = pltpu.VMEM
    dma = pltpu.SemaphoreType.DMA
    anyspace = pl.BlockSpec(memory_space=pl.ANY)
    block = vm((ROWS, COLS), F32)
    scratch = [
        pltpu.SMEM((NH,), F32),
        vm((ROWS, COLS), BF),
        vm((REACH + 1, ROWS, HS), BF),
        vm((REACH + 1, ROWS, HS), BF),
        vm((NH, ROWS), jnp.int32),
        vm((ROWS, COLS), BF),
        vm((1, COLS), F32),
        vm((COLS, 256), BF),
        vm((REACH + 1, HEADS, ROWS, HS), F32),
        vm((HEADS, ROWS, HS), F32),
        vm((HEADS, ROWS, HS), F32),
        vm((NH, ROWS, ROWS), F32),
        vm((NH, ROWS), F32),
        vm((ROWS, COLS), F32),
        vm((ROWS, COLS), F32),
        vm((2, 2, 128), F32),
        vm((NZ, 2, 128), F32),
        vm((NZ, 2, 128), F32),
        vm((ROWS, COLS), BF),
        vm((ROWS, COLS), F32),
        vm((ROWS, COLS), F32),
        vm((2, 2, HALF, 384), F32),
        vm((2, HALF, 384), F32),
        vm((2, HALF, 256), BF),
        vm((2, NY, HALF, 256), BF),
        vm((2, 2, HALF, 256), BF),
        vm((2, HALF, 128), F32),
        vm((2, NY, HALF, 128), F32),
        vm((2, 2, HALF, 128), BF),
        vm((4, NZ, SLICE, 128), BF),
        vm((4, NZ, SLICE, 128), BF),
        vm((2, NZ, SLICE, 128), F32),
        vm((4, SLICE + 8, 128), F32),
        vm((4, NX, SLICE + 8, 128), F32),
        vm((4, NZ, SLICE, 128), BF),
        vm((4, NZ, SLICE, 128), BF),
        vm((8, 128), F32),
        vm((NT, 8, 128), F32),
        dma((8,)),
        dma((2, REACH + 1)), dma((2, REACH + 1)),
        dma, dma,
        dma((2,)), dma((2,)), dma((2,)), dma((2,)), dma((2,)), dma((2,)),
        dma((2,)), dma((2,)), dma((2,)), dma((2,)),
        dma((4,)), dma((4,)), dma((4,)), dma((4,)), dma((4,)), dma((4,)),
        dma, dma,
    ]
    return pl.pallas_call(
        kernel,
        out_shape=(block, block),
        in_specs=[anyspace] * 8,
        out_specs=(pl.BlockSpec(memory_space=vm),) * 2,
        scratch_shapes=scratch,
        compiler_params=pltpu.CompilerParams(
            collective_id=0, has_side_effects=True, vmem_limit_bytes=60 << 20
        ),
    )(queries, rotated_keys, values, decay_rates, decay_codes.T, gate_input, norm_gain, bc_weight)


def solution(mesh):
    return jax.shard_map(
        on_device,
        mesh=mesh,
        in_specs=(
            P("seq", "tp"),
            P("seq", "tp"),
            P("seq", "tp"),
            P("tp"),
            P("seq", "tp"),
            P("seq", "tp"),
            P("tp"),
            P("tp", None),
        ),
        out_specs=(P("seq", "tp"), P("seq", "tp")),
        check_vma=False,
    )
```

```python
import functools
import math

import jax
import jax.numpy as jnp
from jax import lax
from jax.experimental import pallas as pl
from jax.experimental.pallas import tpu as pltpu
from jax.sharding import PartitionSpec as P

HEADS = 4
HS = 128
NH = 8
PAIRS = NH // 2
ROWS = 128
REACH = 16
NZ = 16
NX = 4
NT = 8
NY = 4
HALF = 64
CHANNELS = 4096
COLS = 512
NS = 128
EPS = 1e-5
SLICE = 16
BF = jnp.bfloat16
F32 = jnp.float32
MESH = pl.DeviceIdType.MESH
NEG = -1e30
FIRST = (3, 13, 1, 15, 16)
RELAY = {3: (6, 4, 2), 13: (10, 14, 12), 6: (8, 7, 5), 10: (9, 11)}
NEAR = (1, 2, 3, 13, 15)


def dot(a, b, ca=1, cb=0):
    return lax.dot_general(a, b, (((ca,), (cb,)), ((), ())), preferred_element_type=F32)


def split(a):
    hi = a.astype(BF).astype(F32)
    return hi, a - hi


def pack4(a, b, lane):
    ah, al = split(a)
    bh, bl = split(b)
    return jnp.where(lane < 64, jnp.where(lane < 32, ah, al), jnp.where(lane < 96, bh, bl))


def unpack4(v):
    return v[:, 0:1] + v[:, 32:33], v[:, 64:65] + v[:, 96:97]


def kernel(
    q_hbm, k_hbm, v_hbm, rates_hbm, codes_hbm, gate_hbm, gain_hbm, w_hbm,
    out1, out2,
    rates, q_s, k_s, v_s, codes_s, gate_s, gain_s, w_s,
    sc_s, p_s, m_s, l_s, decay_s, tail_s, expell_s, silu_s,
    dexp_s, dz_s, dp_s,
    x_s, gated_s, y_s,
    pay_s, pr_s, ysrc_s, rs_s, ag_s, csrc_s, cs_s, agc_s,
    cb_s, e1_s, pre_s, tsrc_s, t_s, e3src_s, st_s,
    gsrc_s, g_s,
    in_sem,
    kv_ss, kv_rs, d_ss, d_rs,
    pair_ss, pair_rs, rs_ss, rs_rs, ag_ss, ag_rs, cs_ss, cs_rs, agc_ss, agc_rs,
    e1_ss, e1_rs, t_ss, t_rs, e3_ss, e3_rs,
    g_ss, g_rs,
):
    s = lax.axis_index("seq")
    t = lax.axis_index("tp")
    x = lax.div(s, NZ)
    z = lax.rem(s, NZ)
    chip = lax.div(t, 2)
    core = lax.rem(t, 2)
    partner = (s, t + 1 - 2 * core)

    def zpeer(j):
        o = lax.rem(z + j, NZ)
        return o, (x * NZ + o, t)

    def xpeer(j):
        o = lax.rem(x + j, NX)
        return o, (o * NZ + z, t)

    def tpeer(j):
        o = lax.rem(t + j, NT)
        return o, (s, o)

    def ypeer(j):
        o = lax.rem(chip + j, NY)
        return o, (s, 2 * o + core)

    def remote(src, dst, ss, rs, dev):
        return pltpu.make_async_remote_copy(
            src_ref=src, dst_ref=dst, send_sem=ss, recv_sem=rs, device_id=dev, device_id_type=MESH
        )

    def all_in(ref, sem):
        remote(ref, ref, sem, sem, partner).wait_recv()

    def all_out(ref, sem):
        remote(ref, ref, sem, sem, partner).wait_send()

    def each(n, body):
        body(n // 2)

        def step(j, c):
            body(n // 2 - j)
            body(n // 2 + j)
            return c

        lax.fori_loop(1, n // 2, step, 0)

    barrier = pltpu.get_barrier_semaphore()

    def greet(dev):
        pl.semaphore_signal(barrier, inc=1, device_id=dev, device_id_type=MESH)

    def block_device(k):
        return (lax.rem(s + (k + NX * NZ), NX * NZ), t)

    each(NZ, lambda j: greet(zpeer(j)[1]))
    for k in NEAR:
        greet(block_device(k))
        greet(block_device(-k))
    each(NX, lambda j: greet(xpeer(j)[1]))
    each(NT, lambda j: greet(tpeer(j)[1]))

    loads = [
        pltpu.make_async_copy(src, dst, in_sem.at[i])
        for i, (src, dst) in enumerate(
            (
                (k_hbm, k_s.at[0]),
                (v_hbm, v_s.at[0]),
                (codes_hbm, codes_s),
                (rates_hbm, rates),
                (q_hbm, q_s),
                (gate_hbm, gate_s),
                (gain_hbm, gain_s.at[0]),
                (w_hbm, w_s),
            )
        )
    ]
    for c in loads:
        c.start()

    pl.semaphore_wait(barrier, 2 * len(NEAR) + (NX - 1) + (NZ - 1) + (NT - 1))

    def hop(i, a, b):
        buf = (k_s, v_s)[i]
        return remote(buf.at[a], buf.at[b], kv_ss.at[i, b], kv_rs.at[i, b], block_device(b - a))

    def arrived(i, b):
        hop(i, b - 1, b).wait_recv()

    loads[0].wait()
    loads[1].wait()
    for group in (FIRST[:2], FIRST[2:]):
        for i in range(2):
            for b in group:
                hop(i, 0, b).start()

    row = lax.broadcasted_iota(jnp.int32, (ROWS, ROWS), 0)
    col = lax.broadcasted_iota(jnp.int32, (ROWS, ROWS), 1)
    lane1 = lax.broadcasted_iota(jnp.int32, (1, 128), 1)
    lower = row >= col
    upper = jnp.where(row <= col, 1.0, 0.0).astype(BF)
    loads[2].wait()
    loads[3].wait()
    codes = codes_s[...]
    code_hi = lax.shift_right_logical(codes, 7).astype(F32).astype(BF)
    code_lo = (codes & 127).astype(F32).astype(BF)
    cum_rows = dot(code_hi, upper) * 128.0 + dot(code_lo, upper)
    cum = jnp.transpose(jnp.concatenate([cum_rows, jnp.zeros((128 - NH, ROWS), F32)], 0))
    for hp in range(PAIRS):
        ells, ends = [], []
        for h in (2 * hp, 2 * hp + 1):
            rate = -rates[h]
            ell = cum[:, h : h + 1] * rate
            ell_row = cum_rows[h : h + 1, :] * rate
            end = ell[ROWS - 1 :, :]
            gap = jnp.where(lower, ell - ell_row, 0.0)
            decay_s[h] = jnp.where(lower, jnp.exp(gap), 0.0)
            tail_s[h : h + 1, :] = jnp.exp(end - ell_row)
            ells.append(jnp.exp(ell))
            ends.append(jnp.exp(end))
        cs = slice(hp * 128, hp * 128 + 128)
        expell_s[:, cs] = jnp.where(col < 64, ells[0], ells[1])
        dexp_s[hp % 2, hp // 2 : hp // 2 + 1, :] = jnp.where(lane1 < 64, ends[0], ends[1])

    def d_send(j):
        o, dev = zpeer(j)
        remote(dexp_s.at[lax.div(o, 8)], dz_s.at[z], d_ss, d_rs, dev).start()

    each(NZ, d_send)
    dz_s[z] = dexp_s[lax.div(z, 8)]

    loads[4].wait()
    scale = math.log2(math.e) / math.sqrt(HS)
    diff = col - row
    own_k = k_s[0]
    for h in range(HEADS):
        qh = q_s[:, h * HS : (h + 1) * HS]
        sc = jnp.where(lower, dot(qh, own_k, 1, 1), NEG)
        m = jnp.max(sc, axis=1, keepdims=True)
        m_s[h] = jnp.broadcast_to(m, (ROWS, HS))
        l_s[h] = jnp.exp2((sc - m) * scale)
        sc_s[0, h] = sc

    loads[5].wait()
    g = gate_s[...].astype(F32)
    silu_s[...] = g / (1.0 + jnp.exp(-g))

    def decay_products():
        all_in(dz_s.at[pl.ds(0, NZ - 1)], d_rs)
        running = jnp.ones((2, 128), F32)
        for zz in range(NZ):
            dp_s[zz] = running
            running = running * dz_s[zz]
        for p in range(2):
            for half in range(2):
                tsrc_s[2 * p + half, SLICE:] = jnp.broadcast_to(running[half : half + 1], (8, 128))

    def relay(a, b):
        for i in range(2):
            for k in (a, b):
                arrived(i, k)
                hop(i, k, RELAY[k][0]).start()
            for n in (1, 2):
                for k in (a, b):
                    for to in RELAY[k][n : n + 1]:
                        hop(i, k, to).start()

    def come(*slots):
        for b in slots:
            arrived(0, b)

    def attend(a, b):
        big = jnp.int32(1 << 20)

        def limit(k):
            return jnp.where(s >= k, jnp.int32((k - REACH) * ROWS), big)

        keys = jnp.concatenate([k_s[a], k_s[b]], 0)
        ok = jnp.concatenate([diff > limit(a), diff > limit(b)], 1)
        for h in range(HEADS):
            qh = q_s[:, h * HS : (h + 1) * HS]
            sc = jnp.where(ok, dot(qh, keys, 1, 1), NEG)
            old = m_s[h]
            m = jnp.maximum(old, jnp.max(sc, axis=1, keepdims=True))
            alpha = jnp.exp2((old - m) * scale)
            mm = jnp.concatenate([m, m], 1)
            p = jnp.exp2((sc - mm) * scale)
            m_s[h] = m
            l_s[h] = l_s[h] * alpha + (p[:, :HS] + p[:, HS:])
            sc_s[a, h] = sc[:, :HS]
            sc_s[b, h] = sc[:, HS:]

    relay(3, 13)
    come(1, 15)
    attend(1, 15)
    attend(3, 13)
    relay(6, 10)
    come(16, 2, 4, 14, 12)
    attend(2, 16)
    attend(4, 14)
    attend(6, 12)
    come(5)
    attend(5, 10)
    come(7, 11)
    attend(7, 11)
    come(8, 9)
    attend(8, 9)
    decay_products()
    for h in range(HEADS):
        m = m_s[h]
        inv = 1.0 / jnp.sum(l_s[h], axis=1, keepdims=True)
        for k in range(REACH + 1):
            p_s[h, :, k * ROWS : (k + 1) * ROWS] = (
                jnp.exp2((sc_s[k, h] - m) * scale) * inv
            ).astype(BF)
    for k in range(1, REACH + 1):
        if k not in RELAY:
            arrived(1, k)
    window_v = v_s[...].reshape((REACH + 1) * ROWS, HS)
    for h in range(HEADS):
        x_s[:, h * HS : (h + 1) * HS] = dot(p_s[h], window_v).astype(BF)

    loads[6].wait()
    loads[7].wait()

    def kv_done():
        for i in range(2):
            for b in FIRST:
                hop(i, 0, b).wait_send()
            for a, bs in RELAY.items():
                for b in bs:
                    hop(i, a, b).wait_send()

    def pass_done(p):
        pair_copy(p).wait_send()
        share_copy(p, core).wait_send()
        share_c(p, core).wait_send()
        all_out(cs_s.at[p, pl.ds(0, NY - 1)], cs_ss.at[p])
        all_out(rs_s.at[p, pl.ds(0, NY - 1)], rs_ss.at[p])
        for q in (2 * p, 2 * p + 1):
            all_out(e1_s.at[q, pl.ds(0, NZ - 1)], e1_ss.at[q])
            all_out(t_s.at[q, pl.ds(0, NX - 1)], t_ss.at[q])
            all_out(st_s.at[q, pl.ds(0, NZ - 1)], e3_ss.at[q])

    lane_half = lax.broadcasted_iota(jnp.int32, (HALF, 128), 1)

    def e1_copy(q, to, slot):
        o, dev = to
        return remote(cb_s.at[q, o], e1_s.at[q, slot], e1_ss.at[q], e1_rs.at[q], dev)

    def t_copy(q, to, slot):
        o, dev = to
        return remote(tsrc_s.at[q], t_s.at[q, slot], t_ss.at[q], t_rs.at[q], dev)

    def e3_copy(q, to, slot):
        o, dev = to
        return remote(e3src_s.at[q, o], st_s.at[q, slot], e3_ss.at[q], e3_rs.at[q], dev)

    def pair_copy(p):
        return remote(pay_s.at[p, 1 - core], pr_s.at[p], pair_ss.at[p], pair_rs.at[p], partner)

    def y_copy(p, o, dev, slot):
        return remote(ysrc_s.at[p], rs_s.at[p, slot], rs_ss.at[p], rs_rs.at[p], dev)

    def c_copy(p, dev):
        return remote(csrc_s.at[p], cs_s.at[p, chip], cs_ss.at[p], cs_rs.at[p], dev)

    def share_c(p, half):
        return remote(agc_s.at[p, half], agc_s.at[p, half], agc_ss.at[p], agc_rs.at[p], partner)

    def share_copy(p, half):
        return remote(ag_s.at[p, half], ag_s.at[p, half], ag_ss.at[p], ag_rs.at[p], partner)


    for p in range(2):
        if p == 0:
            xb = x_s[...]
            xf = xb.astype(F32)
            s1 = s2 = jnp.sum(xf * xf, axis=1, keepdims=True)
        else:
            gv = gated_s[...]
            s1 = jnp.sum(gv * gv, axis=1, keepdims=True)
            gg = gv * gain_s[...]
            s2 = jnp.sum(gg * gg, axis=1, keepdims=True)
            xb = gg.astype(BF)
        partial = jnp.concatenate([dot(xb, w_s[...]), pack4(s1, s2, col)], 1)
        pay_s[p] = partial.reshape(2, HALF, 384)
        pair = pair_copy(p)
        pair.start()
        pair.wait_recv()
        both = pay_s[p, core] + pr_s[p]
        q1, q2 = unpack4(both[:, 256:])
        mine = jnp.concatenate([both[:, :128], pack4(q1, q2, lane_half)], 1).astype(BF)
        ysrc_s[p] = mine
        rs_s[p, chip] = mine
        each(NY, lambda j, p=p: y_copy(p, ypeer(j)[0], ypeer(j)[1], chip).start())
        csrc_s[p] = both[:, 128:256]
        cs_s[p, chip] = both[:, 128:256]
        each(NY, lambda j, p=p: c_copy(p, ypeer(j)[1]).start())
        all_in(rs_s.at[p, pl.ds(0, NY - 1)], rs_rs.at[p])
        tot = jnp.sum(rs_s[p].astype(F32), axis=0)
        q1, q2 = unpack4(tot[:, 128:])
        if p == 0:
            scale1 = jnp.ones_like(q1)
        else:
            scale1 = jnp.sqrt(q1 * (1.0 / CHANNELS) + EPS)
        spread = jnp.sqrt(q2 / (scale1 * scale1) * (1.0 / CHANNELS) + EPS)
        per_row = 1.0 / (scale1 * spread)
        proj = tot[:, :128] * per_row
        ag_s[p, core] = jnp.concatenate([proj, pack4(scale1, spread, lane_half)], 1).astype(BF)
        share_copy(p, core).start()
        share_copy(p, 1 - core).wait_recv()
        agv = ag_s[p].reshape(ROWS, 256)
        b_in = agv[:, :128]
        scale1, spread = unpack4(agv[:, 128:].astype(F32))
        if p == 1:
            f1 = gated_s[...] * (1.0 / scale1) * gain_s[...]
            out1[...] = f1
            xf = f1.astype(BF).astype(F32)
        xn = (xf * (1.0 / spread)).astype(BF)

        b_wide = jnp.transpose(b_in.astype(F32))
        b_rows = b_wide.astype(BF)
        for half in range(2):
            for hp in (2 * half, 2 * half + 1):
                xp = xn[:, hp * 128 : hp * 128 + 128]
                one, two = [
                    dot((b_wide * tail_s[h : h + 1, :]).astype(BF), xp) for h in (2 * hp, 2 * hp + 1)
                ]
                contrib = jnp.where(col < 64, one, two).astype(BF)
                for nq in range(8):
                    cb_s[2 * p + half, 8 * (hp % 2) + nq] = contrib[nq * SLICE : (nq + 1) * SLICE]
            each(NZ, lambda j, q=2 * p + half: e1_copy(q, zpeer(j), z).start())
            e1_s[2 * p + half, z] = cb_s[2 * p + half, z]

        all_in(cs_s.at[p, pl.ds(0, NY - 1)], cs_rs.at[p])
        agc_s[p, core] = (jnp.sum(cs_s[p], axis=0) * per_row).astype(BF)
        share_c(p, core).start()
        share_c(p, 1 - core).wait_recv()
        c_out = agc_s[p].reshape(ROWS, NS)
        gram = dot(c_out, b_rows)
        for hp in range(PAIRS):
            cs = slice(hp * 128, hp * 128 + 128)
            mix = jnp.concatenate([gram * decay_s[2 * hp], gram * decay_s[2 * hp + 1]], 1).astype(BF)
            xp = xn[:, cs]
            zero = jnp.zeros_like(xp)
            both = jnp.concatenate([jnp.where(col < 64, xp, zero), jnp.where(col < 64, zero, xp)], 0)
            y_s[:, cs] = dot(mix, both)

        if p == 0:
            kv_done()
            all_out(dz_s.at[pl.ds(0, NZ - 1)], d_ss)
        else:
            pass_done(0)
        for half in range(2):
            q = 2 * p + half
            all_in(e1_s.at[q, pl.ds(0, NZ - 1)], e1_rs.at[q])
            state = jnp.zeros((SLICE, 128), F32)
            for zz in range(NZ):
                pre_s[half, zz] = state
                state = dz_s[zz, half : half + 1, :] * state + e1_s[q, zz].astype(F32)
            tsrc_s[q, :SLICE] = state
            t_s[q, x] = tsrc_s[q]
            each(NX, lambda j, q=q: t_copy(q, xpeer(j), x).start())
        for half in range(2):
            q = 2 * p + half
            all_in(t_s.at[q, pl.ds(0, NX - 1)], t_rs.at[q])
            before = jnp.zeros((SLICE, 128), F32)
            for xx in range(NX - 1):
                decay = t_s[q, xx, SLICE : SLICE + 1]
                before = jnp.where(xx < x, decay * before + t_s[q, xx, :SLICE], before)
            for zz in range(NZ):
                e3src_s[q, zz] = (pre_s[half, zz] + dp_s[zz, half : half + 1, :] * before).astype(BF)
            each(NZ, lambda j, q=q: e3_copy(q, zpeer(j), z).start())
            st_s[q, z] = e3src_s[q, z]
        for half in range(2):
            q = 2 * p + half
            all_in(st_s.at[q, pl.ds(0, NZ - 1)], e3_rs.at[q])
            for hp in (2 * half, 2 * half + 1):
                cs = slice(hp * 128, hp * 128 + 128)
                st = st_s[q, 8 * (hp % 2) : 8 * (hp % 2) + 8].reshape(128, 128)
                y = y_s[:, cs] + dot(c_out, st) * expell_s[:, cs]
                gated_s[:, cs] = y * silu_s[:, cs]

    gv = gated_s[...]
    hi, lo = split(gv * gv)
    ones8 = jnp.ones((8, COLS), BF)
    mine = dot(ones8, hi.astype(BF), 1, 1) + dot(ones8, lo.astype(BF), 1, 1)
    gsrc_s[...] = mine
    g_s[t] = mine

    def g_send(j):
        o, dev = tpeer(j)
        remote(gsrc_s, g_s.at[t], g_ss, g_rs, dev).start()

    each(NT, g_send)
    pass_done(1)
    all_in(g_s.at[pl.ds(0, NT - 1)], g_rs)
    total = jnp.sum(g_s[...], axis=0)[0:1, :]
    inv = lax.rsqrt(total * (1.0 / CHANNELS) + EPS)
    inv = jnp.transpose(jnp.broadcast_to(inv, (128, 128)))
    for hp in range(PAIRS):
        cs = slice(hp * 128, hp * 128 + 128)
        out2[:, cs] = gated_s[:, cs] * inv * gain_s[:, cs]
    all_out(g_s.at[pl.ds(0, NT - 1)], g_ss)


def on_device(
    queries, rotated_keys, values, decay_rates, decay_codes, gate_input, norm_gain, bc_weight
):
    vm = pltpu.VMEM
    dma = pltpu.SemaphoreType.DMA
    anyspace = pl.BlockSpec(memory_space=pl.ANY)
    block = vm((ROWS, COLS), F32)
    scratch = [
        pltpu.SMEM((NH,), F32),
        vm((ROWS, COLS), BF),
        vm((REACH + 1, ROWS, HS), BF),
        vm((REACH + 1, ROWS, HS), BF),
        vm((NH, ROWS), jnp.int32),
        vm((ROWS, COLS), BF),
        vm((1, COLS), F32),
        vm((COLS, 256), BF),
        vm((REACH + 1, HEADS, ROWS, HS), F32),
        vm((HEADS, ROWS, (REACH + 1) * ROWS), BF),
        vm((HEADS, ROWS, HS), F32),
        vm((HEADS, ROWS, HS), F32),
        vm((NH, ROWS, ROWS), F32),
        vm((NH, ROWS), F32),
        vm((ROWS, COLS), F32),
        vm((ROWS, COLS), F32),
        vm((2, 2, 128), F32),
        vm((NZ, 2, 128), F32),
        vm((NZ, 2, 128), F32),
        vm((ROWS, COLS), BF),
        vm((ROWS, COLS), F32),
        vm((ROWS, COLS), F32),
        vm((2, 2, HALF, 384), F32),
        vm((2, HALF, 384), F32),
        vm((2, HALF, 256), BF),
        vm((2, NY, HALF, 256), BF),
        vm((2, 2, HALF, 256), BF),
        vm((2, HALF, 128), F32),
        vm((2, NY, HALF, 128), F32),
        vm((2, 2, HALF, 128), BF),
        vm((4, NZ, SLICE, 128), BF),
        vm((4, NZ, SLICE, 128), BF),
        vm((2, NZ, SLICE, 128), F32),
        vm((4, SLICE + 8, 128), F32),
        vm((4, NX, SLICE + 8, 128), F32),
        vm((4, NZ, SLICE, 128), BF),
        vm((4, NZ, SLICE, 128), BF),
        vm((8, 128), F32),
        vm((NT, 8, 128), F32),
        dma((8,)),
        dma((2, REACH + 1)), dma((2, REACH + 1)),
        dma, dma,
        dma((2,)), dma((2,)), dma((2,)), dma((2,)), dma((2,)), dma((2,)),
        dma((2,)), dma((2,)), dma((2,)), dma((2,)),
        dma((4,)), dma((4,)), dma((4,)), dma((4,)), dma((4,)), dma((4,)),
        dma, dma,
    ]
    return pl.pallas_call(
        kernel,
        out_shape=(block, block),
        in_specs=[anyspace] * 8,
        out_specs=(pl.BlockSpec(memory_space=vm),) * 2,
        scratch_shapes=scratch,
        compiler_params=pltpu.CompilerParams(
            collective_id=0, has_side_effects=True, vmem_limit_bytes=60 << 20
        ),
    )(queries, rotated_keys, values, decay_rates, decay_codes.T, gate_input, norm_gain, bc_weight)


def solution(mesh):
    return jax.shard_map(
        on_device,
        mesh=mesh,
        in_specs=(
            P("seq", "tp"),
            P("seq", "tp"),
            P("seq", "tp"),
            P("tp"),
            P("seq", "tp"),
            P("seq", "tp"),
            P("tp"),
            P("tp", None),
        ),
        out_specs=(P("seq", "tp"), P("seq", "tp")),
        check_vma=False,
    )
```

```python
import functools
import math

import jax
import jax.numpy as jnp
from jax import lax
from jax.experimental import pallas as pl
from jax.experimental.pallas import tpu as pltpu
from jax.sharding import PartitionSpec as P

HEADS = 4
HS = 128
NH = 8
PAIRS = NH // 2
ROWS = 128
REACH = 16
NZ = 16
NX = 4
NT = 8
NY = 4
HALF = 64
CHANNELS = 4096
COLS = 512
NS = 128
EPS = 1e-5
SLICE = 16
BF = jnp.bfloat16
F32 = jnp.float32
MESH = pl.DeviceIdType.MESH
NEG = -1e30
FIRST = (3, 13, 1, 15, 16)
RELAY = {3: (6, 4, 2), 13: (10, 14, 12), 6: (8, 7, 5), 10: (9, 11)}
NEAR = (1, 2, 3, 13, 15)


def dot(a, b, ca=1, cb=0):
    return lax.dot_general(a, b, (((ca,), (cb,)), ((), ())), preferred_element_type=F32)


def split(a):
    hi = a.astype(BF).astype(F32)
    return hi, a - hi


def pack4(a, b, lane):
    ah, al = split(a)
    bh, bl = split(b)
    return jnp.where(lane < 64, jnp.where(lane < 32, ah, al), jnp.where(lane < 96, bh, bl))


def unpack4(v):
    return v[:, 0:1] + v[:, 32:33], v[:, 64:65] + v[:, 96:97]


def kernel(
    q_hbm, k_hbm, v_hbm, rates_hbm, codes_hbm, gate_hbm, gain_hbm, w_hbm,
    out1, out2,
    rates, q_s, k_s, v_s, codes_s, gate_s, gain_s, w_s,
    sc_s, p_s, m_s, l_s, decay_s, tail_s, expell_s, silu_s,
    dexp_s, dz_s, dp_s,
    x_s, gated_s, y_s,
    pay_s, pr_s, ysrc_s, rs_s, ag_s, csrc_s, cs_s, agc_s,
    cb_s, e1_s, pre_s, tsrc_s, t_s, e3src_s, st_s,
    gsrc_s, g_s,
    in_sem,
    kv_ss, kv_rs, d_ss, d_rs,
    pair_ss, pair_rs, rs_ss, rs_rs, ag_ss, ag_rs, cs_ss, cs_rs, agc_ss, agc_rs,
    e1_ss, e1_rs, t_ss, t_rs, e3_ss, e3_rs,
    g_ss, g_rs,
):
    s = lax.axis_index("seq")
    t = lax.axis_index("tp")
    x = lax.div(s, NZ)
    z = lax.rem(s, NZ)
    chip = lax.div(t, 2)
    core = lax.rem(t, 2)
    partner = (s, t + 1 - 2 * core)

    def zpeer(j):
        o = lax.rem(z + j, NZ)
        return o, (x * NZ + o, t)

    def xpeer(j):
        o = lax.rem(x + j, NX)
        return o, (o * NZ + z, t)

    def tpeer(j):
        o = lax.rem(t + j, NT)
        return o, (s, o)

    def ypeer(j):
        o = lax.rem(chip + j, NY)
        return o, (s, 2 * o + core)

    def remote(src, dst, ss, rs, dev):
        return pltpu.make_async_remote_copy(
            src_ref=src, dst_ref=dst, send_sem=ss, recv_sem=rs, device_id=dev, device_id_type=MESH
        )

    def all_in(ref, sem):
        remote(ref, ref, sem, sem, partner).wait_recv()

    def all_out(ref, sem):
        remote(ref, ref, sem, sem, partner).wait_send()

    def each(n, body):
        body(n // 2)

        def step(j, c):
            body(n // 2 - j)
            body(n // 2 + j)
            return c

        lax.fori_loop(1, n // 2, step, 0)

    barrier = pltpu.get_barrier_semaphore()

    def greet(dev):
        pl.semaphore_signal(barrier, inc=1, device_id=dev, device_id_type=MESH)

    def block_device(k):
        return (lax.rem(s + (k + NX * NZ), NX * NZ), t)

    each(NZ, lambda j: greet(zpeer(j)[1]))
    for k in NEAR:
        greet(block_device(k))
        greet(block_device(-k))
    each(NX, lambda j: greet(xpeer(j)[1]))
    each(NT, lambda j: greet(tpeer(j)[1]))

    loads = [
        pltpu.make_async_copy(src, dst, in_sem.at[i])
        for i, (src, dst) in enumerate(
            (
                (k_hbm, k_s.at[0]),
                (v_hbm, v_s.at[0]),
                (codes_hbm, codes_s),
                (rates_hbm, rates),
                (q_hbm, q_s),
                (gate_hbm, gate_s),
                (gain_hbm, gain_s.at[0]),
                (w_hbm, w_s),
            )
        )
    ]
    for c in loads:
        c.start()

    pl.semaphore_wait(barrier, 2 * len(NEAR) + (NX - 1) + (NZ - 1) + (NT - 1))

    def hop(i, a, b):
        buf = (k_s, v_s)[i]
        return remote(buf.at[a], buf.at[b], kv_ss.at[i, b], kv_rs.at[i, b], block_device(b - a))

    def arrived(i, b):
        hop(i, b - 1, b).wait_recv()

    loads[0].wait()
    loads[1].wait()
    for group in (FIRST[:2], FIRST[2:]):
        for i in range(2):
            for b in group:
                hop(i, 0, b).start()

    row = lax.broadcasted_iota(jnp.int32, (ROWS, ROWS), 0)
    col = lax.broadcasted_iota(jnp.int32, (ROWS, ROWS), 1)
    lane1 = lax.broadcasted_iota(jnp.int32, (1, 128), 1)
    lower = row >= col
    upper = jnp.where(row <= col, 1.0, 0.0).astype(BF)
    loads[2].wait()
    loads[3].wait()
    codes = codes_s[...]
    code_hi = lax.shift_right_logical(codes, 7).astype(F32).astype(BF)
    code_lo = (codes & 127).astype(F32).astype(BF)
    cum_rows = dot(code_hi, upper) * 128.0 + dot(code_lo, upper)
    cum = jnp.transpose(jnp.concatenate([cum_rows, jnp.zeros((128 - NH, ROWS), F32)], 0))
    for hp in range(PAIRS):
        ells, ends = [], []
        for h in (2 * hp, 2 * hp + 1):
            rate = -rates[h]
            ell = cum[:, h : h + 1] * rate
            ell_row = cum_rows[h : h + 1, :] * rate
            end = ell[ROWS - 1 :, :]
            gap = jnp.where(lower, ell - ell_row, 0.0)
            decay_s[h] = jnp.where(lower, jnp.exp(gap), 0.0)
            tail_s[h : h + 1, :] = jnp.exp(end - ell_row)
            ells.append(jnp.exp(ell))
            ends.append(jnp.exp(end))
        cs = slice(hp * 128, hp * 128 + 128)
        expell_s[:, cs] = jnp.where(col < 64, ells[0], ells[1])
        dexp_s[hp % 2, hp // 2 : hp // 2 + 1, :] = jnp.where(lane1 < 64, ends[0], ends[1])

    def d_send(j):
        o, dev = zpeer(j)
        remote(dexp_s.at[lax.div(o, 8)], dz_s.at[z], d_ss, d_rs, dev).start()

    each(NZ, d_send)
    dz_s[z] = dexp_s[lax.div(z, 8)]

    def decay_products():
        all_in(dz_s.at[pl.ds(0, NZ - 1)], d_rs)
        running = jnp.ones((2, 128), F32)
        for zz in range(NZ):
            dp_s[zz] = running
            running = running * dz_s[zz]
        for p in range(2):
            for half in range(2):
                tsrc_s[2 * p + half, SLICE:] = jnp.broadcast_to(running[half : half + 1], (8, 128))

    def relay(a, b):
        for i in range(2):
            for k in (a, b):
                arrived(i, k)
                hop(i, k, RELAY[k][0]).start()
            for n in (1, 2):
                for k in (a, b):
                    for to in RELAY[k][n : n + 1]:
                        hop(i, k, to).start()

    def come(*slots):
        for b in slots:
            arrived(0, b)

    def attend(a, b):
        big = jnp.int32(1 << 20)

        def limit(k):
            return jnp.where(s >= k, jnp.int32((k - REACH) * ROWS), big)

        keys = jnp.concatenate([k_s[a], k_s[b]], 0)
        ok = jnp.concatenate([diff > limit(a), diff > limit(b)], 1)
        for h in range(HEADS):
            qh = q_s[:, h * HS : (h + 1) * HS]
            sc = jnp.where(ok, dot(qh, keys, 1, 1), NEG)
            old = m_s[h]
            m = jnp.maximum(old, jnp.max(sc, axis=1, keepdims=True))
            alpha = jnp.exp2((old - m) * scale)
            mm = jnp.concatenate([m, m], 1)
            p = jnp.exp2((sc - mm) * scale)
            m_s[h] = m
            l_s[h] = l_s[h] * alpha + (p[:, :HS] + p[:, HS:])
            sc_s[a, h] = sc[:, :HS]
            sc_s[b, h] = sc[:, HS:]

    relay(3, 13)
    loads[4].wait()
    scale = math.log2(math.e) / math.sqrt(HS)
    diff = col - row
    own_k = k_s[0]
    for h in range(HEADS):
        qh = q_s[:, h * HS : (h + 1) * HS]
        sc = jnp.where(lower, dot(qh, own_k, 1, 1), NEG)
        m = jnp.max(sc, axis=1, keepdims=True)
        m_s[h] = jnp.broadcast_to(m, (ROWS, HS))
        l_s[h] = jnp.exp2((sc - m) * scale)
        sc_s[0, h] = sc

    loads[5].wait()
    g = gate_s[...].astype(F32)
    silu_s[...] = g / (1.0 + jnp.exp(-g))


    come(1, 15)
    attend(1, 15)
    attend(3, 13)
    relay(6, 10)
    come(16, 2, 4, 14, 12)
    attend(2, 16)
    attend(4, 14)
    attend(6, 12)
    come(5)
    attend(5, 10)
    come(7, 11)
    attend(7, 11)
    come(8, 9)
    attend(8, 9)
    decay_products()
    for h in range(HEADS):
        m = m_s[h]
        inv = 1.0 / jnp.sum(l_s[h], axis=1, keepdims=True)
        for k in range(REACH + 1):
            p_s[h, :, k * ROWS : (k + 1) * ROWS] = (
                jnp.exp2((sc_s[k, h] - m) * scale) * inv
            ).astype(BF)
    for k in range(1, REACH + 1):
        if k not in RELAY:
            arrived(1, k)
    window_v = v_s[...].reshape((REACH + 1) * ROWS, HS)
    for h in range(HEADS):
        x_s[:, h * HS : (h + 1) * HS] = dot(p_s[h], window_v).astype(BF)

    loads[6].wait()
    loads[7].wait()

    def kv_done():
        for i in range(2):
            for b in FIRST:
                hop(i, 0, b).wait_send()
            for a, bs in RELAY.items():
                for b in bs:
                    hop(i, a, b).wait_send()

    def pass_done(p):
        pair_copy(p).wait_send()
        share_copy(p, core).wait_send()
        share_c(p, core).wait_send()
        all_out(cs_s.at[p, pl.ds(0, NY - 1)], cs_ss.at[p])
        all_out(rs_s.at[p, pl.ds(0, NY - 1)], rs_ss.at[p])
        for q in (2 * p, 2 * p + 1):
            all_out(e1_s.at[q, pl.ds(0, NZ - 1)], e1_ss.at[q])
            all_out(t_s.at[q, pl.ds(0, NX - 1)], t_ss.at[q])
            all_out(st_s.at[q, pl.ds(0, NZ - 1)], e3_ss.at[q])

    lane_half = lax.broadcasted_iota(jnp.int32, (HALF, 128), 1)

    def e1_copy(q, to, slot):
        o, dev = to
        return remote(cb_s.at[q, o], e1_s.at[q, slot], e1_ss.at[q], e1_rs.at[q], dev)

    def t_copy(q, to, slot):
        o, dev = to
        return remote(tsrc_s.at[q], t_s.at[q, slot], t_ss.at[q], t_rs.at[q], dev)

    def e3_copy(q, to, slot):
        o, dev = to
        return remote(e3src_s.at[q, o], st_s.at[q, slot], e3_ss.at[q], e3_rs.at[q], dev)

    def pair_copy(p):
        return remote(pay_s.at[p, 1 - core], pr_s.at[p], pair_ss.at[p], pair_rs.at[p], partner)

    def y_copy(p, o, dev, slot):
        return remote(ysrc_s.at[p], rs_s.at[p, slot], rs_ss.at[p], rs_rs.at[p], dev)

    def c_copy(p, dev):
        return remote(csrc_s.at[p], cs_s.at[p, chip], cs_ss.at[p], cs_rs.at[p], dev)

    def share_c(p, half):
        return remote(agc_s.at[p, half], agc_s.at[p, half], agc_ss.at[p], agc_rs.at[p], partner)

    def share_copy(p, half):
        return remote(ag_s.at[p, half], ag_s.at[p, half], ag_ss.at[p], ag_rs.at[p], partner)


    for p in range(2):
        if p == 0:
            xb = x_s[...]
            xf = xb.astype(F32)
            s1 = s2 = jnp.sum(xf * xf, axis=1, keepdims=True)
        else:
            gv = gated_s[...]
            s1 = jnp.sum(gv * gv, axis=1, keepdims=True)
            gg = gv * gain_s[...]
            s2 = jnp.sum(gg * gg, axis=1, keepdims=True)
            xb = gg.astype(BF)
        partial = jnp.concatenate([dot(xb, w_s[...]), pack4(s1, s2, col)], 1)
        pay_s[p] = partial.reshape(2, HALF, 384)
        pair = pair_copy(p)
        pair.start()
        pair.wait_recv()
        both = pay_s[p, core] + pr_s[p]
        q1, q2 = unpack4(both[:, 256:])
        mine = jnp.concatenate([both[:, :128], pack4(q1, q2, lane_half)], 1).astype(BF)
        ysrc_s[p] = mine
        rs_s[p, chip] = mine
        each(NY, lambda j, p=p: y_copy(p, ypeer(j)[0], ypeer(j)[1], chip).start())
        csrc_s[p] = both[:, 128:256]
        cs_s[p, chip] = both[:, 128:256]
        all_in(rs_s.at[p, pl.ds(0, NY - 1)], rs_rs.at[p])
        each(NY, lambda j, p=p: c_copy(p, ypeer(j)[1]).start())
        tot = jnp.sum(rs_s[p].astype(F32), axis=0)
        q1, q2 = unpack4(tot[:, 128:])
        if p == 0:
            scale1 = jnp.ones_like(q1)
        else:
            scale1 = jnp.sqrt(q1 * (1.0 / CHANNELS) + EPS)
        spread = jnp.sqrt(q2 / (scale1 * scale1) * (1.0 / CHANNELS) + EPS)
        per_row = 1.0 / (scale1 * spread)
        proj = tot[:, :128] * per_row
        ag_s[p, core] = jnp.concatenate([proj, pack4(scale1, spread, lane_half)], 1).astype(BF)
        share_copy(p, core).start()
        share_copy(p, 1 - core).wait_recv()
        agv = ag_s[p].reshape(ROWS, 256)
        b_in = agv[:, :128]
        scale1, spread = unpack4(agv[:, 128:].astype(F32))
        if p == 1:
            f1 = gated_s[...] * (1.0 / scale1) * gain_s[...]
            out1[...] = f1
            xf = f1.astype(BF).astype(F32)
        xn = (xf * (1.0 / spread)).astype(BF)

        b_wide = jnp.transpose(b_in.astype(F32))
        b_rows = b_wide.astype(BF)
        for half in range(2):
            for hp in (2 * half, 2 * half + 1):
                xp = xn[:, hp * 128 : hp * 128 + 128]
                one, two = [
                    dot((b_wide * tail_s[h : h + 1, :]).astype(BF), xp) for h in (2 * hp, 2 * hp + 1)
                ]
                contrib = jnp.where(col < 64, one, two).astype(BF)
                for nq in range(8):
                    cb_s[2 * p + half, 8 * (hp % 2) + nq] = contrib[nq * SLICE : (nq + 1) * SLICE]
            each(NZ, lambda j, q=2 * p + half: e1_copy(q, zpeer(j), z).start())
            e1_s[2 * p + half, z] = cb_s[2 * p + half, z]

        all_in(cs_s.at[p, pl.ds(0, NY - 1)], cs_rs.at[p])
        agc_s[p, core] = (jnp.sum(cs_s[p], axis=0) * per_row).astype(BF)
        share_c(p, core).start()
        share_c(p, 1 - core).wait_recv()
        c_out = agc_s[p].reshape(ROWS, NS)
        gram = dot(c_out, b_rows)
        for hp in range(PAIRS):
            cs = slice(hp * 128, hp * 128 + 128)
            mix = jnp.concatenate([gram * decay_s[2 * hp], gram * decay_s[2 * hp + 1]], 1).astype(BF)
            xp = xn[:, cs]
            zero = jnp.zeros_like(xp)
            both = jnp.concatenate([jnp.where(col < 64, xp, zero), jnp.where(col < 64, zero, xp)], 0)
            y_s[:, cs] = dot(mix, both)

        if p == 0:
            kv_done()
            all_out(dz_s.at[pl.ds(0, NZ - 1)], d_ss)
        else:
            pass_done(0)
        for half in range(2):
            q = 2 * p + half
            all_in(e1_s.at[q, pl.ds(0, NZ - 1)], e1_rs.at[q])
            state = jnp.zeros((SLICE, 128), F32)
            for zz in range(NZ):
                pre_s[half, zz] = state
                state = dz_s[zz, half : half + 1, :] * state + e1_s[q, zz].astype(F32)
            tsrc_s[q, :SLICE] = state
            t_s[q, x] = tsrc_s[q]
            each(NX, lambda j, q=q: t_copy(q, xpeer(j), x).start())
        for half in range(2):
            q = 2 * p + half
            all_in(t_s.at[q, pl.ds(0, NX - 1)], t_rs.at[q])
            before = jnp.zeros((SLICE, 128), F32)
            for xx in range(NX - 1):
                decay = t_s[q, xx, SLICE : SLICE + 1]
                before = jnp.where(xx < x, decay * before + t_s[q, xx, :SLICE], before)
            for zz in range(NZ):
                e3src_s[q, zz] = (pre_s[half, zz] + dp_s[zz, half : half + 1, :] * before).astype(BF)
            each(NZ, lambda j, q=q: e3_copy(q, zpeer(j), z).start())
            st_s[q, z] = e3src_s[q, z]
        for half in range(2):
            q = 2 * p + half
            all_in(st_s.at[q, pl.ds(0, NZ - 1)], e3_rs.at[q])
            for hp in (2 * half, 2 * half + 1):
                cs = slice(hp * 128, hp * 128 + 128)
                st = st_s[q, 8 * (hp % 2) : 8 * (hp % 2) + 8].reshape(128, 128)
                y = y_s[:, cs] + dot(c_out, st) * expell_s[:, cs]
                gated_s[:, cs] = y * silu_s[:, cs]

    gv = gated_s[...]
    hi, lo = split(gv * gv)
    ones8 = jnp.ones((8, COLS), BF)
    mine = dot(ones8, hi.astype(BF), 1, 1) + dot(ones8, lo.astype(BF), 1, 1)
    gsrc_s[...] = mine
    g_s[t] = mine

    def g_send(j):
        o, dev = tpeer(j)
        remote(gsrc_s, g_s.at[t], g_ss, g_rs, dev).start()

    each(NT, g_send)
    pass_done(1)
    all_in(g_s.at[pl.ds(0, NT - 1)], g_rs)
    total = jnp.sum(g_s[...], axis=0)[0:1, :]
    inv = lax.rsqrt(total * (1.0 / CHANNELS) + EPS)
    inv = jnp.transpose(jnp.broadcast_to(inv, (128, 128)))
    for hp in range(PAIRS):
        cs = slice(hp * 128, hp * 128 + 128)
        out2[:, cs] = gated_s[:, cs] * inv * gain_s[:, cs]
    all_out(g_s.at[pl.ds(0, NT - 1)], g_ss)


def on_device(
    queries, rotated_keys, values, decay_rates, decay_codes, gate_input, norm_gain, bc_weight
):
    vm = pltpu.VMEM
    dma = pltpu.SemaphoreType.DMA
    anyspace = pl.BlockSpec(memory_space=pl.ANY)
    block = vm((ROWS, COLS), F32)
    scratch = [
        pltpu.SMEM((NH,), F32),
        vm((ROWS, COLS), BF),
        vm((REACH + 1, ROWS, HS), BF),
        vm((REACH + 1, ROWS, HS), BF),
        vm((NH, ROWS), jnp.int32),
        vm((ROWS, COLS), BF),
        vm((1, COLS), F32),
        vm((COLS, 256), BF),
        vm((REACH + 1, HEADS, ROWS, HS), F32),
        vm((HEADS, ROWS, (REACH + 1) * ROWS), BF),
        vm((HEADS, ROWS, HS), F32),
        vm((HEADS, ROWS, HS), F32),
        vm((NH, ROWS, ROWS), F32),
        vm((NH, ROWS), F32),
        vm((ROWS, COLS), F32),
        vm((ROWS, COLS), F32),
        vm((2, 2, 128), F32),
        vm((NZ, 2, 128), F32),
        vm((NZ, 2, 128), F32),
        vm((ROWS, COLS), BF),
        vm((ROWS, COLS), F32),
        vm((ROWS, COLS), F32),
        vm((2, 2, HALF, 384), F32),
        vm((2, HALF, 384), F32),
        vm((2, HALF, 256), BF),
        vm((2, NY, HALF, 256), BF),
        vm((2, 2, HALF, 256), BF),
        vm((2, HALF, 128), F32),
        vm((2, NY, HALF, 128), F32),
        vm((2, 2, HALF, 128), BF),
        vm((4, NZ, SLICE, 128), BF),
        vm((4, NZ, SLICE, 128), BF),
        vm((2, NZ, SLICE, 128), F32),
        vm((4, SLICE + 8, 128), F32),
        vm((4, NX, SLICE + 8, 128), F32),
        vm((4, NZ, SLICE, 128), BF),
        vm((4, NZ, SLICE, 128), BF),
        vm((8, 128), F32),
        vm((NT, 8, 128), F32),
        dma((8,)),
        dma((2, REACH + 1)), dma((2, REACH + 1)),
        dma, dma,
        dma((2,)), dma((2,)), dma((2,)), dma((2,)), dma((2,)), dma((2,)),
        dma((2,)), dma((2,)), dma((2,)), dma((2,)),
        dma((4,)), dma((4,)), dma((4,)), dma((4,)), dma((4,)), dma((4,)),
        dma, dma,
    ]
    return pl.pallas_call(
        kernel,
        out_shape=(block, block),
        in_specs=[anyspace] * 8,
        out_specs=(pl.BlockSpec(memory_space=vm),) * 2,
        scratch_shapes=scratch,
        compiler_params=pltpu.CompilerParams(
            collective_id=0, has_side_effects=True, vmem_limit_bytes=60 << 20
        ),
    )(queries, rotated_keys, values, decay_rates, decay_codes.T, gate_input, norm_gain, bc_weight)


def solution(mesh):
    return jax.shard_map(
        on_device,
        mesh=mesh,
        in_specs=(
            P("seq", "tp"),
            P("seq", "tp"),
            P("seq", "tp"),
            P("tp"),
            P("seq", "tp"),
            P("seq", "tp"),
            P("tp"),
            P("tp", None),
        ),
        out_specs=(P("seq", "tp"), P("seq", "tp")),
        check_vma=False,
    )
```
